32 devices in a mesh: sec: 2 (over x), dev: 16 (over z, y, core).
Axes of the slice: x: 2, y: 2, z: 4, core: 2. Of those that a mesh axis runs over, the one named last changes fastest.
Arguments:
- queries: bfloat16 [32, 8192], P('dev', 'sec'), may hold values from -24 to 24
- cache_keys: bfloat16 [32, 4, 512, 128], P('dev', 'sec'), may hold values from -24 to 24
- cache_values: bfloat16 [32, 4, 512, 128], P('dev', 'sec'), may hold values from -48 to 48
- lengths: int32 [32], P('dev'), may hold values from 2 to 512, as said below
- out_proj: bfloat16 [4096, 8192], P('dev', 'sec'), may hold values from -0.0625 to 0.0625
- residual: bfloat16 [32, 4096], P(None, 'dev'), may hold values from -3 to 3
- norm_gain: bfloat16 [4096], replicated, may hold values from 0.5 to 1.5
- expert_ids: int32 [32, 8], replicated, may hold values from 0 to 15, all different within a row; in each aligned block of 32 rows (0 to 31, 32 to 63, ...) at most 32 rows name the same one
- gate_weights: float32 [32, 8], replicated, may hold values from 0.5 to 1.5
- owners: int32 [16], replicated, may hold values from 0 to 15, each once
- gate_proj: bfloat16 [16, 768, 4096], P('dev', 'sec'), may hold values from -0.09375 to 0.09375
- up_proj: bfloat16 [16, 768, 4096], P('dev', 'sec'), may hold values from -0.09375 to 0.09375
- down_proj: bfloat16 [16, 768, 4096], P('dev', 'sec'), may hold values from -0.21875 to 0.21875
Outputs:
- output: bfloat16 [32, 4096], P(None, 'dev')
The draws below stay inside these ranges and needn't reach their ends.
Inputs may be any that keep to these rules, and one draw needn't show every extreme that they name: Row r's cache holds lengths[r] live positions from position 0; some row holds exactly 512. `expert_ids`: each row names 8 different experts; over all 32 rows no expert is named more than 32 times, a bound that some block reaches. Each index appears once; expert e's projections stand at index owners[e] of the expert projections.
All inputs are finite; a program needn't handle non-finite values.
Results may differ from the reference program's by a relative error of at most 0.009.
Values may be sent and summed in bfloat16 or wider, within the bound.
A program may use at most 64 MiB of HBM per device.

```python
import math
import jax
import jax.numpy as jnp
import numpy as np
from jax import lax

D = 4096
HEADS = 64
KV_HEADS = 4
HEAD_DIM = 128
TOPK = 8
FF_WIN = 768
CACHE = 512
EXPERTS = 16
ROWS = 32
CAP = 32


def draw_queries(key, part):
    baseline = jnp.clip(jax.random.normal(jax.random.fold_in(key, 11), (ROWS, HEADS * HEAD_DIM), jnp.float32), -6.0, 6.0)
    return baseline.astype(jnp.bfloat16)


def draw_cache_keys(key, part):
    baseline = jnp.clip(jax.random.normal(jax.random.fold_in(key, 23), (ROWS, KV_HEADS, CACHE, HEAD_DIM), jnp.float32), -6.0, 6.0)
    return baseline.astype(jnp.bfloat16)


def draw_lengths(key, part):
    subkeys = jax.random.split(jax.random.fold_in(key, 31), 3)
    lengths_out = jax.random.randint(subkeys[0], (ROWS,), 2, CACHE + 1, dtype=jnp.int32)
    longest = jax.random.randint(subkeys[1], (), 0, ROWS, dtype=jnp.int32)
    offset = jax.random.randint(subkeys[2], (), 1, ROWS, dtype=jnp.int32)
    shortest = (longest + offset) % ROWS
    return lengths_out.at[longest].set(CACHE).at[shortest].set(2)


def block_scale(key, extent, cuts, low, largest):
    factor_of, own = 1.0, jax.random.fold_in(key, 6)
    for dim, shards_of in cuts:
        draws = jnp.exp(jax.random.uniform(jax.random.fold_in(own, dim), (shards_of,), jnp.float32, low / len(cuts), largest / len(cuts)))
        factor_of = factor_of * jnp.repeat(draws, extent[dim] // shards_of).reshape([-1 if axis == dim else 1 for axis in range(len(extent))])
    return factor_of


def routed_block(rng, own, number, rows, amount, top, most, slope):
    ranking = jax.random.permutation(rng, amount)
    crowded, usual = shares(amount, rows * top, most, slope, True), shares(amount, rows * top, most, slope, False)
    places = jnp.arange(amount)

    def named(sizes, rotation):
        used = int((sizes > 0).sum())
        fixed = max(1, used // 4)
        shifted = fixed + (places - fixed + rotation * (used - fixed)) % max(1, amount - fixed)
        return jnp.zeros((amount,), jnp.int32).at[ranking[jnp.where(places < fixed, places, shifted)]].set(jnp.asarray(sizes, jnp.int32))

    sizes = jnp.where(number % 4 == 0, named(crowded, number // 4), named(usual, number - number // 4 - 1))
    mixed = jax.random.permutation(jax.random.fold_in(own, 3), amount)
    giver, taker = mixed[0:amount // 2 * 2:2], mixed[1:amount // 2 * 2:2]
    slack = jnp.minimum(sizes[giver] - 1, most - sizes[taker]) // 2
    slack = jnp.where((giver == ranking[0]) | (taker == ranking[0]) | (sizes[taker] == 0), 0, jnp.maximum(slack, 0))
    shifted = jax.random.randint(jax.random.fold_in(own, 4), (amount // 2,), 0, 1 << 20) % (slack + 1)
    sizes = sizes.at[giver].add(-shifted).at[taker].add(shifted)
    items = jnp.searchsorted(jnp.cumsum(sizes), jnp.arange(rows * top), side="right").astype(jnp.int32)
    grid = items.reshape(top, rows).T
    grid = grid[jax.random.permutation(jax.random.fold_in(own, 1), rows)]
    rotation = jax.random.randint(jax.random.fold_in(own, 2), (rows, 1), 0, top)
    return jnp.take_along_axis(grid, (jnp.arange(top)[None, :] + rotation) % top, axis=1)


def shares(count, total, bound, skew, full):
    loads = [(1 << 20) // math.isqrt(standing ** skew) + 1 for standing in range(1, count + 1)]
    largest = bound if full else min(bound, max(-(-total // count), total * loads[0] // sum(loads)))
    least = 1 if total - largest >= count - 1 else 0
    holding, rest = [largest] + [least] * (count - 1), total - largest - least * (count - 1)
    while rest > 0:
        movable = [i for i in range(1, count) if holding[i] < largest] or [i for i in range(1, count) if holding[i] < bound]
        pool, budget = sum([loads[i] for i in movable]), rest
        for i in movable:
            more = min(bound - holding[i], max(1, budget * loads[i] // pool), rest)
            holding[i] = holding[i] + more
            rest = rest - more
    return np.array(holding)


def gaussian(key, shape, deviation, bound, cuts=(), kind=jnp.bfloat16):
    array = deviation * jax.random.normal(key, shape, jnp.float32)
    if cuts:
        array = array * block_scale(key, shape, cuts, -0.22, 0.18)
    return jnp.clip(array, -bound, bound).astype(kind)


def setup_inputs(seed: int = 0) -> dict:
    keys = jax.random.split(jax.random.key(seed), 14)
    queries = draw_queries(jax.random.fold_in(keys[13], 71), 0)
    cache_keys = draw_cache_keys(jax.random.fold_in(keys[13], 71), 0)
    cache_values = gaussian(keys[2], (ROWS, KV_HEADS, CACHE, HEAD_DIM), 8.0, 48.0, ((0, 16), (1, 2)))
    lengths = draw_lengths(jax.random.fold_in(keys[13], 71), 0)
    out_proj = gaussian(keys[4], (D, HEADS * HEAD_DIM), (HEADS * HEAD_DIM) ** -0.5, 0.0625, ((0, 16), (1, 2)))
    residual = gaussian(keys[5], (ROWS, D), 0.5, 3.0, ((1, 16),))
    norm_gain = jnp.clip(1.0 + 0.1 * jax.random.normal(keys[6], (D,), jnp.float32), 0.5, 1.5).astype(jnp.bfloat16)
    expert_ids_keys = jax.random.split(jax.random.fold_in(keys[7], 1), ROWS // ROWS)
    expert_ids_turns = jax.random.permutation(jax.random.fold_in(keys[7], 3), ROWS // ROWS)
    expert_ids = jax.vmap(lambda own, number: routed_block(jax.random.fold_in(keys[7], 2), own, number, ROWS, EXPERTS, TOPK, CAP, 2))(expert_ids_keys, expert_ids_turns).reshape((ROWS, TOPK))
    gate_weights = jnp.clip(jax.random.uniform(keys[8], (ROWS, TOPK), jnp.float32, 0.5, 1.5), 0.5, 1.5)
    owners = jax.random.permutation(keys[9], EXPERTS).astype(jnp.int32)
    gate_proj = gaussian(keys[10], (EXPERTS, FF_WIN, D), D ** -0.5, 0.09375, ((0, 16), (1, 2)))
    up_proj = gaussian(keys[11], (EXPERTS, FF_WIN, D), D ** -0.5, 0.09375, ((0, 16), (1, 2)))
    down_proj = gaussian(keys[12], (EXPERTS, FF_WIN, D), FF_WIN ** -0.5, 0.21875, ((0, 16), (1, 2)))
    return dict(queries=queries, cache_keys=cache_keys, cache_values=cache_values, lengths=lengths, out_proj=out_proj, residual=residual, norm_gain=norm_gain, expert_ids=expert_ids, gate_weights=gate_weights, owners=owners, gate_proj=gate_proj, up_proj=up_proj, down_proj=down_proj)


epsilon = 1e-05

def slot_targets(expert_ids, owners, capacity):
    experts = owners.shape[0]
    flat_ids = expert_ids.reshape(-1)
    one_hot = (flat_ids[:, None] == jnp.arange(experts, dtype=jnp.int32)[None, :]).astype(jnp.int32)
    before = jnp.cumsum(one_hot, axis=0) - one_hot
    position = lax.optimization_barrier(jnp.sum(before * one_hot, axis=1))
    holder = lax.optimization_barrier(jnp.sum(one_hot * owners[None, :], axis=1))
    return (holder * capacity + position).reshape(expert_ids.shape)

def routing_tables(expert_ids, gate_weights, owners, capacity):
    target = slot_targets(expert_ids, owners, capacity)
    places = jnp.arange(owners.shape[0] * capacity, dtype=jnp.int32)
    matched = target[None, :, :] == places[:, None, None]
    sending = jnp.any(matched, axis=2)
    weighting = lax.optimization_barrier(jnp.sum(jnp.where(matched, gate_weights[None, :, :], jnp.zeros_like(gate_weights)[None, :, :]), axis=2))
    return (sending, weighting)

def times_transpose(left, right):
    return lax.dot_general(left, right, (((1,), (1,)), ((), ())), preferred_element_type=jnp.float32)

def attend(queries, cache_keys, cache_values, lengths):
    rows, kv_heads, key_span, head_dim = cache_keys.shape
    group_size = queries.shape[1] // (kv_heads * head_dim)
    grouped = queries.reshape(rows, kv_heads, group_size, head_dim)
    scores = jnp.einsum('rkgd,rktd->rkgt', grouped.astype(jnp.float32), cache_keys.astype(jnp.float32)) / math.sqrt(head_dim)
    live_mask = jnp.arange(key_span, dtype=jnp.int32)[None, None, None, :] < lengths[:, None, None, None]
    scores = jnp.where(live_mask, scores, -jnp.inf)
    row_top = lax.optimization_barrier(jnp.max(scores, axis=-1, keepdims=True))
    raised = jnp.exp(scores - row_top)
    soft_weight = (raised / lax.optimization_barrier(jnp.sum(raised, axis=-1, keepdims=True))).astype(jnp.bfloat16)
    head_out = jnp.einsum('rkgt,rktd->rkgd', soft_weight.astype(jnp.float32), cache_values.astype(jnp.float32))
    return head_out.astype(jnp.bfloat16).reshape(rows, -1)

def root_norm(arrived, norm_gain):
    square_mean = lax.optimization_barrier(jnp.mean(arrived * arrived, axis=-1, keepdims=True))
    return (arrived * lax.rsqrt(square_mean + epsilon) * norm_gain.astype(arrived.dtype)).astype(jnp.bfloat16)

def expert_ffn(normed, gate_w, up_w, down_w):
    gate_act = times_transpose(normed, gate_w)
    up_act = times_transpose(normed, up_w)
    hidden = (jax.nn.silu(gate_act) * up_act).astype(jnp.bfloat16)
    return jnp.dot(hidden, down_w, preferred_element_type=jnp.float32)

def expert_packed(packed):
    return expert_ffn(packed[0], packed[1], packed[2], packed[3])

def reference(queries, cache_keys, cache_values, lengths, out_proj, residual, norm_gain, expert_ids, gate_weights, owners, gate_proj, up_proj, down_proj):
    head_out = attend(queries, cache_keys, cache_values, lengths)
    attention_out = times_transpose(head_out, out_proj)
    hidden_in = (residual.astype(jnp.float32) + attention_out).astype(jnp.bfloat16)
    sending, weighting = routing_tables(expert_ids, gate_weights, owners, CAP)
    arrived = jnp.dot(sending.astype(jnp.bfloat16), hidden_in, preferred_element_type=jnp.float32)
    normed = root_norm(arrived, norm_gain).reshape(EXPERTS, CAP, D)
    expert_out = lax.map(expert_packed, (normed, gate_proj, up_proj, down_proj)).reshape(EXPERTS * CAP, D)
    place_weight = lax.optimization_barrier(jnp.sum(weighting, axis=1))
    weighted = (expert_out * place_weight[:, None]).astype(jnp.bfloat16)
    moe = jnp.dot(sending.T.astype(jnp.bfloat16), weighted, preferred_element_type=jnp.float32)
    return (residual.astype(jnp.float32) + attention_out + moe).astype(jnp.bfloat16)
```

```python
import functools
import math

import jax
import jax.numpy as jnp
from jax import lax
from jax.experimental import pallas as pl
from jax.experimental.pallas import tpu as pltpu
from jax.sharding import PartitionSpec as P

epsilon = 1e-05
MESH = pl.DeviceIdType.MESH


def slot_targets(expert_ids, owners, capacity):
    experts = owners.shape[0]
    flat_ids = expert_ids.reshape(-1)
    one_hot = (flat_ids[:, None] == jnp.arange(experts, dtype=jnp.int32)[None, :]).astype(jnp.int32)
    before = jnp.cumsum(one_hot, axis=0) - one_hot
    position = jnp.sum(before * one_hot, axis=1)
    holder = jnp.sum(one_hot * owners[None, :], axis=1)
    return (holder * capacity + position).reshape(expert_ids.shape)


def routing_tables(expert_ids, gate_weights, owners, capacity):
    target = slot_targets(expert_ids, owners, capacity)
    places = jnp.arange(owners.shape[0] * capacity, dtype=jnp.int32)
    matched = target[None, :, :] == places[:, None, None]
    sending = jnp.any(matched, axis=2)
    weighting = jnp.sum(
        jnp.where(matched, gate_weights[None, :, :], jnp.zeros_like(gate_weights)[None, :, :]),
        axis=2,
    )
    return (sending, weighting)


def times_transpose(left, right):
    return lax.dot_general(
        left, right, (((1,), (1,)), ((), ())), preferred_element_type=jnp.float32
    )


def attend(queries, cache_keys, cache_values, lengths):
    rows, kv_heads, key_span, head_dim = cache_keys.shape
    group_size = queries.shape[1] // (kv_heads * head_dim)
    grouped = queries.reshape(rows, kv_heads, group_size, head_dim)
    scores = jnp.einsum(
        "rkgd,rktd->rkgt", grouped, cache_keys, preferred_element_type=jnp.float32
    ) / math.sqrt(head_dim)
    live_mask = (
        jnp.arange(key_span, dtype=jnp.int32)[None, None, None, :] < lengths[:, None, None, None]
    )
    scores = jnp.where(live_mask, scores, -jnp.inf)
    row_top = jnp.max(scores, axis=-1, keepdims=True)
    raised = jnp.exp(scores - row_top)
    soft_weight = (raised / jnp.sum(raised, axis=-1, keepdims=True)).astype(jnp.bfloat16)
    head_out = jnp.einsum(
        "rkgt,rktd->rkgd", soft_weight, cache_values, preferred_element_type=jnp.float32
    )
    return head_out.astype(jnp.bfloat16).reshape(rows, -1)


def root_norm(arrived, norm_gain):
    square_mean = jnp.mean(arrived * arrived, axis=-1, keepdims=True)
    return (arrived * lax.rsqrt(square_mean + epsilon) * norm_gain.astype(jnp.float32)).astype(
        jnp.bfloat16
    )


def expert_ffn(normed, gate_w, up_w, down_w):
    gate_act = times_transpose(normed, gate_w)
    up_act = times_transpose(normed, up_w)
    hidden = (jax.nn.silu(gate_act) * up_act).astype(jnp.bfloat16)
    return jnp.dot(hidden, down_w, preferred_element_type=jnp.float32)


def shards(
    queries,
    cache_keys,
    cache_values,
    lengths,
    out_proj,
    residual,
    norm_gain,
    expert_ids,
    gate_weights,
    owners,
    gate_proj,
    up_proj,
    down_proj,
):
    head_out = attend(queries, cache_keys, cache_values, lengths)
    attention_part = times_transpose(lax.all_gather(head_out, "dev", axis=0, tiled=True), out_proj)
    rows_all, top_count = expert_ids.shape
    experts = owners.shape[0]
    capacity = min(rows_all, 3 * top_count * rows_all // experts)
    col_count = out_proj.shape[0]
    sending, weighting = routing_tables(expert_ids, gate_weights, owners, capacity)
    residual_wide = residual.astype(jnp.float32)
    attention_out = lax.psum(attention_part, "sec")
    hidden_in = (residual_wide + attention_out).astype(jnp.bfloat16)
    outbound = jnp.dot(sending.astype(jnp.bfloat16), hidden_in, preferred_element_type=jnp.float32)
    outbound = outbound.astype(jnp.bfloat16).reshape(experts, capacity, col_count)
    inbound = lax.all_to_all(outbound, "dev", split_axis=0, concat_axis=2, tiled=True)
    arrived = inbound[0].astype(jnp.float32)
    normed = root_norm(arrived, norm_gain)
    expert_out = expert_ffn(normed, gate_proj[0], up_proj[0], down_proj[0])
    place_weight = jnp.sum(weighting, axis=1)
    own_weight = lax.dynamic_slice_in_dim(
        place_weight, lax.axis_index("dev") * capacity, capacity, 0
    )
    weighted = (expert_out * own_weight[:, None]).astype(jnp.bfloat16)
    returned = lax.all_to_all(
        weighted.reshape(1, capacity, weighted.shape[1]),
        "dev",
        split_axis=2,
        concat_axis=0,
        tiled=True,
    )
    moe = jnp.dot(
        sending.T.astype(jnp.bfloat16),
        returned.reshape(-1, col_count),
        preferred_element_type=jnp.float32,
    )
    summed = lax.psum(moe, "sec")
    return (residual_wide + attention_out + summed).astype(jnp.bfloat16)


def fused_kernel(
    n_dev,
    queries,
    lengths,
    residual,
    norm_gain,
    expert_ids,
    gate_weights,
    owners,
    keys_hbm,
    values_hbm,
    out_proj_hbm,
    gate_hbm,
    up_hbm,
    down_hbm,
    output,
    keys,
    values,
    out_proj,
    gate_w,
    up_w,
    down_w,
    query_rows,
    heads_out,
    heads_in,
    heads_wide,
    part_out,
    part_in,
    hidden_out,
    hidden_in,
    back_out,
    back_in,
    last_out,
    last_in,
    load_sem,
    send_sem,
    recv_sem,
    pair_sem,
):
    sec = lax.axis_index("sec")
    dev = lax.axis_index("dev")
    rows_here, kv_heads, span, head_dim = keys.shape
    group = query_rows.shape[1] // rows_here
    rows = n_dev * rows_here
    cols = out_proj.shape[0]
    kv_width = group * head_dim

    loads = [
        pltpu.make_async_copy(source, target, load_sem.at[i])
        for i, (source, target) in enumerate(
            (
                (keys_hbm, keys),
                (values_hbm, values),
                (out_proj_hbm, out_proj),
                (gate_hbm.at[0], gate_w),
                (up_hbm.at[0], up_w),
                (down_hbm.at[0], down_w),
            )
        )
    ]
    for load in loads:
        load.start()

    barrier = pltpu.get_barrier_semaphore()
    pair = {"sec": 1 - sec}
    pl.semaphore_signal(barrier, inc=1, device_id=pair, device_id_type=MESH)

    @pl.loop(1, n_dev)
    def _(step):
        peer = lax.rem(dev + step, n_dev)
        pl.semaphore_signal(barrier, inc=1, device_id={"dev": peer}, device_id_type=MESH)

    def exchange(phase, source_of, target_of):
        @pl.loop(1, n_dev)
        def _(step):
            peer = lax.rem(dev + step, n_dev)
            pltpu.make_async_remote_copy(
                src_ref=source_of(peer),
                dst_ref=target_of(dev),
                send_sem=send_sem.at[phase, peer],
                recv_sem=recv_sem.at[phase, dev],
                device_id={"dev": peer},
                device_id_type=MESH,
            ).start()

    def settle(phase, source_of, target_of, sent):
        @pl.loop(1, n_dev)
        def _(step):
            peer = lax.rem(dev + step, n_dev)
            copy = pltpu.make_async_remote_copy(
                src_ref=source_of(peer),
                dst_ref=target_of(peer),
                send_sem=send_sem.at[phase, peer],
                recv_sem=recv_sem.at[phase, peer],
                device_id={"dev": peer},
                device_id_type=MESH,
            )
            if sent:
                copy.wait_send()
            else:
                copy.wait_recv()

    def across(phase, source, target):
        copy = pltpu.make_async_remote_copy(
            src_ref=source,
            dst_ref=target,
            send_sem=pair_sem.at[phase, 0],
            recv_sem=pair_sem.at[phase, 1],
            device_id=pair,
            device_id_type=MESH,
        )
        copy.start()
        return copy

    wide_queries = queries[...].astype(jnp.float32)
    for row in range(rows_here):
        for kv in range(kv_heads):
            for g in range(group):
                start = (kv * group + g) * head_dim
                query_rows[kv, row * group + g : row * group + g + 1, :] = wide_queries[
                    row : row + 1, start : start + head_dim
                ]
    loads[0].wait()
    loads[1].wait()
    position = lax.broadcasted_iota(jnp.int32, (group, span), 1)
    for row in range(rows_here):
        live = position < lengths[row]
        for kv in range(kv_heads):
            query = query_rows[kv, row * group : (row + 1) * group, :].astype(jnp.bfloat16)
            scores = times_transpose(query, keys[row, kv]) * (1.0 / math.sqrt(head_dim))
            scores = jnp.where(live, scores, -jnp.inf)
            raised = jnp.exp(scores - jnp.max(scores, axis=1, keepdims=True))
            probs = (raised / jnp.sum(raised, axis=1, keepdims=True)).astype(jnp.bfloat16)
            found = jnp.dot(probs, values[row, kv], preferred_element_type=jnp.float32)
            found = found.astype(jnp.bfloat16)
            heads_out[kv * rows_here + row] = found
            heads_in[dev, kv * rows_here + row] = found

    pl.semaphore_wait(barrier, n_dev)
    exchange(0, lambda peer: heads_out, lambda peer: heads_in.at[peer])

    named = jnp.int32(0)
    for e in range(owners.shape[0]):
        named = named + jnp.where(owners[e] == dev, jnp.int32(e), jnp.int32(0))
    weight = jnp.sum(
        jnp.where(expert_ids[...] == named, gate_weights[...], 0.0), axis=1, keepdims=True
    )

    settle(0, lambda peer: heads_out, lambda peer: heads_in.at[peer], False)
    loads[2].wait()
    part = jnp.zeros((rows, cols), jnp.float32)
    for kv in range(kv_heads):
        for d in range(n_dev):
            for row in range(rows_here):
                place = (d * rows_here + row) * group
                heads_wide[place : place + group, :] = heads_in[d, kv * rows_here + row].astype(
                    jnp.float32
                )
        features = jnp.concatenate(
            [heads_wide[pl.ds(g, rows, stride=group), :] for g in range(group)], axis=1
        ).astype(jnp.bfloat16)
        part = part + times_transpose(
            features, out_proj[:, kv * kv_width : (kv + 1) * kv_width]
        )
    part_out[...] = part
    swap = across(0, part_out, part_in)
    swap.wait_recv()
    base = residual[...].astype(jnp.float32) + (part + part_in[...])
    hidden = base.astype(jnp.bfloat16)
    hidden_out[...] = hidden
    hidden_in[dev] = hidden
    exchange(1, lambda peer: hidden_out, lambda peer: hidden_in.at[peer])
    settle(1, lambda peer: hidden_out, lambda peer: hidden_in.at[peer], False)

    arrived = jnp.concatenate([hidden_in[d] for d in range(n_dev)], axis=1).astype(jnp.float32)
    square_mean = jnp.mean(arrived * arrived, axis=1, keepdims=True)
    normed = (
        arrived * lax.rsqrt(square_mean + epsilon) * norm_gain[...].astype(jnp.float32)
    ).astype(jnp.bfloat16)
    loads[3].wait()
    loads[4].wait()
    gate_act = times_transpose(normed, gate_w[...])
    up_act = times_transpose(normed, up_w[...])
    act = (gate_act * (1.0 / (1.0 + jnp.exp(-gate_act))) * up_act).astype(jnp.bfloat16)
    loads[5].wait()
    for d in range(n_dev):
        made = jnp.dot(
            act, down_w[:, d * cols : (d + 1) * cols], preferred_element_type=jnp.float32
        )
        back_out[d] = (made * weight).astype(jnp.bfloat16)
    exchange(2, lambda peer: back_out.at[peer], lambda peer: back_in.at[peer])
    back_in[dev] = back_out[dev]
    settle(2, lambda peer: back_out.at[peer], lambda peer: back_in.at[peer], False)
    moe = back_in[0].astype(jnp.float32)
    for d in range(1, n_dev):
        moe = moe + back_in[d].astype(jnp.float32)
    last_out[...] = moe
    last = across(1, last_out, last_in)
    last.wait_recv()
    output[...] = (base + (moe + last_in[...])).astype(jnp.bfloat16)

    settle(0, lambda peer: heads_out, lambda peer: heads_in.at[peer], True)
    settle(1, lambda peer: hidden_out, lambda peer: hidden_in.at[peer], True)
    settle(2, lambda peer: back_out.at[peer], lambda peer: back_in.at[peer], True)
    swap.wait_send()
    last.wait_send()


def fused(
    n_dev,
    queries,
    cache_keys,
    cache_values,
    lengths,
    out_proj,
    residual,
    norm_gain,
    expert_ids,
    gate_weights,
    owners,
    gate_proj,
    up_proj,
    down_proj,
):
    rows_here, kv_heads, span, head_dim = cache_keys.shape
    cols = out_proj.shape[0]
    rows, width = residual.shape[0], norm_gain.shape[0]
    group = queries.shape[1] // (kv_heads * head_dim)
    units = gate_proj.shape[1]
    vmem = pl.BlockSpec(memory_space=pltpu.VMEM)
    smem = pl.BlockSpec(memory_space=pltpu.SMEM)
    whole = pl.BlockSpec(memory_space=pl.ANY)
    wide, narrow = jnp.float32, jnp.bfloat16
    blocks = rows_here * kv_heads
    return pl.pallas_call(
        functools.partial(fused_kernel, n_dev),
        out_shape=jax.ShapeDtypeStruct((rows, cols), narrow),
        in_specs=[vmem, smem, vmem, vmem, vmem, vmem, smem] + [whole] * 6,
        out_specs=vmem,
        scratch_shapes=[
            pltpu.VMEM(cache_keys.shape, narrow),
            pltpu.VMEM(cache_values.shape, narrow),
            pltpu.VMEM(out_proj.shape, narrow),
            pltpu.VMEM((units, width), narrow),
            pltpu.VMEM((units, width), narrow),
            pltpu.VMEM((units, width), narrow),
            pltpu.VMEM((kv_heads, rows_here * group, head_dim), wide),
            pltpu.VMEM((blocks, group, head_dim), narrow),
            pltpu.VMEM((n_dev, blocks, group, head_dim), narrow),
            pltpu.VMEM((rows * group, head_dim), wide),
            pltpu.VMEM((rows, cols), wide),
            pltpu.VMEM((rows, cols), wide),
            pltpu.VMEM((rows, cols), narrow),
            pltpu.VMEM((n_dev, rows, cols), narrow),
            pltpu.VMEM((n_dev, rows, cols), narrow),
            pltpu.VMEM((n_dev, rows, cols), narrow),
            pltpu.VMEM((rows, cols), wide),
            pltpu.VMEM((rows, cols), wide),
            pltpu.SemaphoreType.DMA((6,)),
            pltpu.SemaphoreType.DMA((3, n_dev)),
            pltpu.SemaphoreType.DMA((3, n_dev)),
            pltpu.SemaphoreType.DMA((2, 2)),
        ],
        compiler_params=pltpu.CompilerParams(
            collective_id=0, has_side_effects=True, vmem_limit_bytes=48 * 1024 * 1024
        ),
        cost_estimate=pl.CostEstimate(
            flops=2 * rows * width * (width + 3 * units),
            bytes_accessed=2 * width * (width + 3 * units),
            transcendentals=0,
        ),
    )(
        queries,
        lengths,
        residual,
        norm_gain.reshape(1, width),
        expert_ids,
        gate_weights,
        owners,
        cache_keys,
        cache_values,
        out_proj,
        gate_proj,
        up_proj,
        down_proj,
    )


def tiles_whole(mesh, operands):
    queries, cache_keys, _, _, out_proj, residual = operands[:6]
    owners, gate_proj = operands[9], operands[10]
    group = queries.shape[1] // (cache_keys.shape[1] * cache_keys.shape[3])
    return (
        mesh.shape["sec"] == 2
        and owners.shape[0] == mesh.shape["dev"]
        and gate_proj.shape[0] == 1
        and group % 16 == 0
        and cache_keys.shape[3] % 128 == 0
        and cache_keys.shape[2] % 128 == 0
        and residual.shape[0] % 16 == 0
        and out_proj.shape[0] % 128 == 0
        and gate_proj.shape[1] % 128 == 0
    )


def solution(mesh):
    in_specs = (
        P("dev", "sec"),
        P("dev", "sec", None, None),
        P("dev", "sec", None, None),
        P("dev"),
        P("dev", "sec"),
        P(None, "dev"),
        P(),
        P(),
        P(),
        P(),
        P("dev", "sec", None),
        P("dev", "sec", None),
        P("dev", "sec", None),
    )
    out_specs = P(None, "dev")

    def chosen(*operands):
        if tiles_whole(mesh, operands):
            return fused(mesh.shape["dev"], *operands)
        return shards(*operands)

    return jax.shard_map(chosen, mesh=mesh, in_specs=in_specs, out_specs=out_specs, check_vma=False)
```

```python
import functools
import math

import jax
import jax.numpy as jnp
from jax import lax
from jax.experimental import pallas as pl
from jax.experimental.pallas import tpu as pltpu
from jax.sharding import PartitionSpec as P

epsilon = 1e-05
MESH = pl.DeviceIdType.MESH


def slot_targets(expert_ids, owners, capacity):
    experts = owners.shape[0]
    flat_ids = expert_ids.reshape(-1)
    one_hot = (flat_ids[:, None] == jnp.arange(experts, dtype=jnp.int32)[None, :]).astype(jnp.int32)
    before = jnp.cumsum(one_hot, axis=0) - one_hot
    position = jnp.sum(before * one_hot, axis=1)
    holder = jnp.sum(one_hot * owners[None, :], axis=1)
    return (holder * capacity + position).reshape(expert_ids.shape)


def routing_tables(expert_ids, gate_weights, owners, capacity):
    target = slot_targets(expert_ids, owners, capacity)
    places = jnp.arange(owners.shape[0] * capacity, dtype=jnp.int32)
    matched = target[None, :, :] == places[:, None, None]
    sending = jnp.any(matched, axis=2)
    weighting = jnp.sum(
        jnp.where(matched, gate_weights[None, :, :], jnp.zeros_like(gate_weights)[None, :, :]),
        axis=2,
    )
    return (sending, weighting)


def times_transpose(left, right):
    return lax.dot_general(
        left, right, (((1,), (1,)), ((), ())), preferred_element_type=jnp.float32
    )


def attend(queries, cache_keys, cache_values, lengths):
    rows, kv_heads, key_span, head_dim = cache_keys.shape
    group_size = queries.shape[1] // (kv_heads * head_dim)
    grouped = queries.reshape(rows, kv_heads, group_size, head_dim)
    scores = jnp.einsum(
        "rkgd,rktd->rkgt", grouped, cache_keys, preferred_element_type=jnp.float32
    ) / math.sqrt(head_dim)
    live_mask = (
        jnp.arange(key_span, dtype=jnp.int32)[None, None, None, :] < lengths[:, None, None, None]
    )
    scores = jnp.where(live_mask, scores, -jnp.inf)
    row_top = jnp.max(scores, axis=-1, keepdims=True)
    raised = jnp.exp(scores - row_top)
    soft_weight = (raised / jnp.sum(raised, axis=-1, keepdims=True)).astype(jnp.bfloat16)
    head_out = jnp.einsum(
        "rkgt,rktd->rkgd", soft_weight, cache_values, preferred_element_type=jnp.float32
    )
    return head_out.astype(jnp.bfloat16).reshape(rows, -1)


def root_norm(arrived, norm_gain):
    square_mean = jnp.mean(arrived * arrived, axis=-1, keepdims=True)
    return (arrived * lax.rsqrt(square_mean + epsilon) * norm_gain.astype(jnp.float32)).astype(
        jnp.bfloat16
    )


def expert_ffn(normed, gate_w, up_w, down_w):
    gate_act = times_transpose(normed, gate_w)
    up_act = times_transpose(normed, up_w)
    hidden = (jax.nn.silu(gate_act) * up_act).astype(jnp.bfloat16)
    return jnp.dot(hidden, down_w, preferred_element_type=jnp.float32)


def shards(
    queries,
    cache_keys,
    cache_values,
    lengths,
    out_proj,
    residual,
    norm_gain,
    expert_ids,
    gate_weights,
    owners,
    gate_proj,
    up_proj,
    down_proj,
):
    head_out = attend(queries, cache_keys, cache_values, lengths)
    attention_part = times_transpose(lax.all_gather(head_out, "dev", axis=0, tiled=True), out_proj)
    rows_all, top_count = expert_ids.shape
    experts = owners.shape[0]
    capacity = min(rows_all, 3 * top_count * rows_all // experts)
    col_count = out_proj.shape[0]
    sending, weighting = routing_tables(expert_ids, gate_weights, owners, capacity)
    residual_wide = residual.astype(jnp.float32)
    attention_out = lax.psum(attention_part, "sec")
    hidden_in = (residual_wide + attention_out).astype(jnp.bfloat16)
    outbound = jnp.dot(sending.astype(jnp.bfloat16), hidden_in, preferred_element_type=jnp.float32)
    outbound = outbound.astype(jnp.bfloat16).reshape(experts, capacity, col_count)
    inbound = lax.all_to_all(outbound, "dev", split_axis=0, concat_axis=2, tiled=True)
    arrived = inbound[0].astype(jnp.float32)
    normed = root_norm(arrived, norm_gain)
    expert_out = expert_ffn(normed, gate_proj[0], up_proj[0], down_proj[0])
    place_weight = jnp.sum(weighting, axis=1)
    own_weight = lax.dynamic_slice_in_dim(
        place_weight, lax.axis_index("dev") * capacity, capacity, 0
    )
    weighted = (expert_out * own_weight[:, None]).astype(jnp.bfloat16)
    returned = lax.all_to_all(
        weighted.reshape(1, capacity, weighted.shape[1]),
        "dev",
        split_axis=2,
        concat_axis=0,
        tiled=True,
    )
    moe = jnp.dot(
        sending.T.astype(jnp.bfloat16),
        returned.reshape(-1, col_count),
        preferred_element_type=jnp.float32,
    )
    summed = lax.psum(moe, "sec")
    return (residual_wide + attention_out + summed).astype(jnp.bfloat16)
VMEM_LIMIT = 64 * 1024 * 1024 - 64 * 1024


def fused_kernel(
    n_dev,
    queries_hbm,
    lengths_hbm,
    residual_hbm,
    gain_hbm,
    ids_hbm,
    router_hbm,
    owners_hbm,
    keys_hbm,
    values_hbm,
    out_proj_hbm,
    gate_hbm,
    up_hbm,
    down_hbm,
    output,
    queries,
    lengths,
    residual,
    gain,
    ids,
    router,
    owners,
    keys,
    values,
    out_proj,
    rising,
    down_w,
    query_rows,
    heads_in,
    heads_wide,
    part_out,
    part_in,
    hidden_in,
    cross_out,
    cross_in,
    back_out,
    back_in,
    last_out,
    last_in,
    load_sem,
    send_sem,
    recv_sem,
    pass_sem,
    back_send_sem,
    back_recv_sem,
    pair_sem,
):
    sec = lax.axis_index("sec")
    dev = lax.axis_index("dev")
    chip, core = lax.div(dev, 2), lax.rem(dev, 2)
    chips = n_dev // 2
    rows_here, kv_heads, span, head_dim = keys.shape
    group = query_rows.shape[1] // rows_here
    rows = n_dev * rows_here
    cols = out_proj.shape[0]
    units = down_w.shape[0]
    kv_width = group * head_dim

    def flipped(k):
        bit, place = 1, 0
        while bit < chips:
            place = place + lax.rem(lax.div(chip, bit) + (k // bit) % 2, 2) * bit
            bit *= 2
        return place

    chip_of = [flipped(k) for k in range(chips)]
    twin = 2 * chip + 1 - core
    to_twin = {"dev": twin}
    across = {"sec": 1 - sec}
    same = [2 * chip_of[k] + core for k in range(chips)]
    other = [2 * chip_of[k] + 1 - core for k in range(chips)]

    pairs = (
        (queries_hbm, queries),
        (keys_hbm, keys),
        (values_hbm, values),
        (lengths_hbm, lengths),
        (out_proj_hbm, out_proj),
        (residual_hbm, residual),
        (gain_hbm, gain),
        (ids_hbm, ids),
        (router_hbm, router),
        (owners_hbm, owners),
        (gate_hbm.at[0], rising.at[pl.ds(0, units)]),
        (up_hbm.at[0], rising.at[pl.ds(units, units)]),
        (down_hbm.at[0], down_w),
    )
    loads = [
        pltpu.make_async_copy(source, target, load_sem.at[i])
        for i, (source, target) in enumerate(pairs)
    ]
    for load in loads:
        load.start()

    barrier = pltpu.get_barrier_semaphore()
    for place in [across, to_twin] + [{"dev": same[k]} for k in range(1, chips)]:
        pl.semaphore_signal(barrier, inc=1, device_id=place, device_id_type=MESH)

    def remote(source, target, sent, received, place):
        return pltpu.make_async_remote_copy(
            src_ref=source,
            dst_ref=target,
            send_sem=sent,
            recv_sem=received,
            device_id=place,
            device_id_type=MESH,
        )

    def landed(phase, buffer, index):
        remote(
            buffer.at[index], buffer.at[index], send_sem.at[phase, 0],
            recv_sem.at[phase, index], to_twin,
        ).wait_recv()

    def gather_start(phase, buffer):
        copies = []
        for k in reversed(range(chips)):
            place = {"dev": same[k]} if k else to_twin
            copies.append(
                remote(
                    buffer.at[dev], buffer.at[dev], send_sem.at[phase, k],
                    recv_sem.at[phase, dev], place,
                )
            )
            copies[-1].start()
        return copies

    def gather_pass(phase, buffer, k):
        landed(phase, buffer, same[k])
        copy = remote(
            buffer.at[same[k]], buffer.at[same[k]], pass_sem.at[phase, k],
            recv_sem.at[phase, same[k]], to_twin,
        )
        copy.start()
        return copy

    loads[0].wait()
    wide_queries = queries[...].astype(jnp.float32)
    for row in range(rows_here):
        for kv in range(kv_heads):
            for g in range(group):
                start = (kv * group + g) * head_dim
                query_rows[kv, row * group + g : row * group + g + 1, :] = wide_queries[
                    row : row + 1, start : start + head_dim
                ]
    loads[1].wait()
    loads[3].wait()
    position = lax.broadcasted_iota(jnp.int32, (group, span), 1)
    scores = []
    for kv in range(kv_heads):
        for row in range(rows_here):
            query = query_rows[kv, row * group : (row + 1) * group, :].astype(jnp.bfloat16)
            found = times_transpose(query, keys[row, kv]) * (1.0 / math.sqrt(head_dim))
            scores.append(jnp.where(position < lengths[row], found, -jnp.inf))
    scores = jnp.concatenate(scores, axis=0)
    raised = jnp.exp(scores - jnp.max(scores, axis=1, keepdims=True))
    probs = (raised / jnp.sum(raised, axis=1, keepdims=True)).astype(jnp.bfloat16)
    loads[2].wait()
    for kv in range(kv_heads):
        for row in range(rows_here):
            block = kv * rows_here + row
            found = jnp.dot(
                probs[block * group : (block + 1) * group],
                values[row, kv],
                preferred_element_type=jnp.float32,
            )
            heads_in[dev, block] = found.astype(jnp.bfloat16)

    pl.semaphore_wait(barrier, chips + 1)
    sends = gather_start(0, heads_in)

    for i in (5, 6, 7, 8, 9):
        loads[i].wait()
    named = jnp.int32(0)
    for e in range(owners.shape[0]):
        named = named + jnp.where(owners[e] == dev, jnp.int32(e), jnp.int32(0))
    lying = jnp.sum(jnp.where(ids[...] == named, router[...], 0.0), axis=0, keepdims=True)
    square = (rows, rows)
    diagonal = lax.broadcasted_iota(jnp.int32, square, 0) == lax.broadcasted_iota(
        jnp.int32, square, 1
    )
    weight = jnp.sum(
        jnp.where(diagonal, jnp.broadcast_to(lying, square), 0.0), axis=1, keepdims=True
    )

    for k in range(1, chips):
        sends.append(gather_pass(0, heads_in, k))
    for k in range(chips):
        landed(0, heads_in, other[k])
    loads[4].wait()
    for kv in range(kv_heads):
        for d in range(n_dev):
            for row in range(rows_here):
                place = (d * rows_here + row) * group
                heads_wide[kv, place : place + group, :] = heads_in[
                    d, kv * rows_here + row
                ].astype(jnp.float32)
    features = jnp.concatenate(
        [
            heads_wide[kv, pl.ds(g, rows, stride=group), :]
            for kv in range(kv_heads)
            for g in range(group)
        ],
        axis=1,
    ).astype(jnp.bfloat16)
    part = times_transpose(features, out_proj[...])
    part_out[...] = part
    swap = remote(part_out, part_in, pair_sem.at[0, 0], pair_sem.at[0, 1], across)
    swap.start()
    sends.append(swap)
    swap.wait_recv()
    base = residual[...].astype(jnp.float32) + (part + part_in[...])
    hidden_in[dev] = base.astype(jnp.bfloat16)
    sends += gather_start(1, hidden_in)

    loads[10].wait()
    loads[11].wait()
    squares = jnp.zeros((rows, cols), jnp.float32)
    raising = jnp.zeros((rows, 2 * units), jnp.float32)

    def take(index, squares, raising):
        start = pl.multiple_of(index * cols, cols)
        block = hidden_in[index].astype(jnp.float32)
        scaled = (block * gain[pl.ds(start, cols)].astype(jnp.float32).reshape(1, cols)).astype(jnp.bfloat16)
        return (
            squares + block * block,
            raising + times_transpose(scaled, rising[:, pl.ds(start, cols)]),
        )

    squares, raising = take(dev, squares, raising)
    for k in range(chips):
        if k:
            sends.append(gather_pass(1, hidden_in, k))
            squares, raising = take(same[k], squares, raising)
        landed(1, hidden_in, other[k])
        squares, raising = take(other[k], squares, raising)
    square_mean = jnp.sum(squares, axis=1, keepdims=True) / (n_dev * cols)
    raising = raising * lax.rsqrt(square_mean + epsilon)
    gate_act, up_act = raising[:, :units], raising[:, units:]
    act = (gate_act * (1.0 / (1.0 + jnp.exp(-gate_act))) * up_act).astype(jnp.bfloat16)

    def lowered(index):
        start = pl.multiple_of(index * cols, cols)
        made = jnp.dot(act, down_w[:, pl.ds(start, cols)], preferred_element_type=jnp.float32)
        return made * weight

    loads[12].wait()
    crossing = {}
    for k in reversed(range(chips)):
        cross_out[k] = lowered(other[k]).astype(jnp.bfloat16)
        crossing[k] = remote(
            cross_out.at[k], cross_in.at[k], back_send_sem.at[0, k], back_recv_sem.at[0, k], to_twin
        )
        crossing[k].start()
        sends.append(crossing[k])
    backs = {}
    for k in reversed(range(chips)):
        made = lowered(same[k])
        crossing[k].wait_recv()
        made = made + cross_in[k].astype(jnp.float32)
        if k == 0:
            moe = made
            continue
        back_out[k] = made.astype(jnp.bfloat16)
        backs[k] = remote(
            back_out.at[k], back_in.at[k], back_send_sem.at[1, k], back_recv_sem.at[1, k],
            {"dev": same[k]},
        )
        backs[k].start()
        sends.append(backs[k])
    for k in range(1, chips):
        backs[k].wait_recv()
        moe = moe + back_in[k].astype(jnp.float32)
    last_out[...] = moe
    last = remote(last_out, last_in, pair_sem.at[1, 0], pair_sem.at[1, 1], across)
    last.start()
    sends.append(last)
    last.wait_recv()
    output[...] = (base + (moe + last_in[...])).astype(jnp.bfloat16)
    for copy in sends:
        copy.wait_send()


def fused(
    n_dev,
    queries,
    cache_keys,
    cache_values,
    lengths,
    out_proj,
    residual,
    norm_gain,
    expert_ids,
    gate_weights,
    owners,
    gate_proj,
    up_proj,
    down_proj,
):
    rows_here, kv_heads, span, head_dim = cache_keys.shape
    cols = out_proj.shape[0]
    rows, width = residual.shape[0], norm_gain.shape[0]
    group = queries.shape[1] // (kv_heads * head_dim)
    units = gate_proj.shape[1]
    chips = n_dev // 2
    whole = pl.BlockSpec(memory_space=pltpu.HBM)
    wide, narrow = jnp.float32, jnp.bfloat16
    blocks = rows_here * kv_heads
    gain = norm_gain
    return pl.pallas_call(
        functools.partial(fused_kernel, n_dev),
        out_shape=jax.ShapeDtypeStruct((rows, cols), narrow),
        in_specs=[whole] * 13,
        out_specs=pl.BlockSpec(memory_space=pltpu.VMEM),
        scratch_shapes=[
            pltpu.VMEM(queries.shape, narrow),
            pltpu.SMEM(lengths.shape, jnp.int32),
            pltpu.VMEM(residual.shape, narrow),
            pltpu.VMEM(gain.shape, narrow),
            pltpu.VMEM(expert_ids.shape[::-1], jnp.int32),
            pltpu.VMEM(gate_weights.shape[::-1], wide),
            pltpu.SMEM(owners.shape, jnp.int32),
            pltpu.VMEM(cache_keys.shape, narrow),
            pltpu.VMEM(cache_values.shape, narrow),
            pltpu.VMEM(out_proj.shape, narrow),
            pltpu.VMEM((2 * units, width), narrow),
            pltpu.VMEM((units, width), narrow),
            pltpu.VMEM((kv_heads, rows_here * group, head_dim), wide),
            pltpu.VMEM((n_dev, blocks, group, head_dim), narrow),
            pltpu.VMEM((kv_heads, rows * group, head_dim), wide),
            pltpu.VMEM((rows, cols), wide),
            pltpu.VMEM((rows, cols), wide),
            pltpu.VMEM((n_dev, rows, cols), narrow),
            pltpu.VMEM((chips, rows, cols), narrow),
            pltpu.VMEM((chips, rows, cols), narrow),
            pltpu.VMEM((chips, rows, cols), narrow),
            pltpu.VMEM((chips, rows, cols), narrow),
            pltpu.VMEM((rows, cols), wide),
            pltpu.VMEM((rows, cols), wide),
            pltpu.SemaphoreType.DMA((13,)),
            pltpu.SemaphoreType.DMA((2, chips)),
            pltpu.SemaphoreType.DMA((2, n_dev)),
            pltpu.SemaphoreType.DMA((2, chips)),
            pltpu.SemaphoreType.DMA((2, chips)),
            pltpu.SemaphoreType.DMA((2, chips)),
            pltpu.SemaphoreType.DMA((2, 2)),
        ],
        compiler_params=pltpu.CompilerParams(
            collective_id=0, has_side_effects=True, vmem_limit_bytes=VMEM_LIMIT
        ),
        cost_estimate=pl.CostEstimate(
            flops=2 * rows * width * (width + 3 * units),
            bytes_accessed=2 * width * (width + 3 * units),
            transcendentals=0,
        ),
    )(
        queries,
        lengths,
        residual,
        gain,
        expert_ids.T,
        gate_weights.T,
        owners,
        cache_keys,
        cache_values,
        out_proj,
        gate_proj,
        up_proj,
        down_proj,
    )


def tiles_whole(mesh, operands):
    queries, cache_keys, _, _, out_proj, residual = operands[:6]
    owners, gate_proj = operands[9], operands[10]
    group = queries.shape[1] // (cache_keys.shape[1] * cache_keys.shape[3])
    return (
        mesh.shape["sec"] == 2
        and mesh.shape["dev"] in (4, 8, 16)
        and owners.shape[0] == mesh.shape["dev"]
        and gate_proj.shape[0] == 1
        and group % 16 == 0
        and cache_keys.shape[3] % 128 == 0
        and cache_keys.shape[2] % 128 == 0
        and residual.shape[0] % 16 == 0
        and out_proj.shape[0] % 128 == 0
        and gate_proj.shape[1] % 128 == 0
    )


def solution(mesh):
    in_specs = (
        P("dev", "sec"),
        P("dev", "sec", None, None),
        P("dev", "sec", None, None),
        P("dev"),
        P("dev", "sec"),
        P(None, "dev"),
        P(),
        P(),
        P(),
        P(),
        P("dev", "sec", None),
        P("dev", "sec", None),
        P("dev", "sec", None),
    )
    out_specs = P(None, "dev")

    def chosen(*operands):
        if tiles_whole(mesh, operands):
            return fused(mesh.shape["dev"], *operands)
        return shards(*operands)

    return jax.shard_map(chosen, mesh=mesh, in_specs=in_specs, out_specs=out_specs, check_vma=False)
```

```python
import functools
import math

import jax
import jax.numpy as jnp
from jax import lax
from jax.experimental import pallas as pl
from jax.experimental.pallas import tpu as pltpu
from jax.sharding import PartitionSpec as P

epsilon = 1e-05
MESH = pl.DeviceIdType.MESH


def slot_targets(expert_ids, owners, capacity):
    experts = owners.shape[0]
    flat_ids = expert_ids.reshape(-1)
    one_hot = (flat_ids[:, None] == jnp.arange(experts, dtype=jnp.int32)[None, :]).astype(jnp.int32)
    before = jnp.cumsum(one_hot, axis=0) - one_hot
    position = jnp.sum(before * one_hot, axis=1)
    holder = jnp.sum(one_hot * owners[None, :], axis=1)
    return (holder * capacity + position).reshape(expert_ids.shape)


def routing_tables(expert_ids, gate_weights, owners, capacity):
    target = slot_targets(expert_ids, owners, capacity)
    places = jnp.arange(owners.shape[0] * capacity, dtype=jnp.int32)
    matched = target[None, :, :] == places[:, None, None]
    sending = jnp.any(matched, axis=2)
    weighting = jnp.sum(
        jnp.where(matched, gate_weights[None, :, :], jnp.zeros_like(gate_weights)[None, :, :]),
        axis=2,
    )
    return (sending, weighting)


def times_transpose(left, right):
    return lax.dot_general(
        left, right, (((1,), (1,)), ((), ())), preferred_element_type=jnp.float32
    )


def attend(queries, cache_keys, cache_values, lengths):
    rows, kv_heads, key_span, head_dim = cache_keys.shape
    group_size = queries.shape[1] // (kv_heads * head_dim)
    grouped = queries.reshape(rows, kv_heads, group_size, head_dim)
    scores = jnp.einsum(
        "rkgd,rktd->rkgt", grouped, cache_keys, preferred_element_type=jnp.float32
    ) / math.sqrt(head_dim)
    live_mask = (
        jnp.arange(key_span, dtype=jnp.int32)[None, None, None, :] < lengths[:, None, None, None]
    )
    scores = jnp.where(live_mask, scores, -jnp.inf)
    row_top = jnp.max(scores, axis=-1, keepdims=True)
    raised = jnp.exp(scores - row_top)
    soft_weight = (raised / jnp.sum(raised, axis=-1, keepdims=True)).astype(jnp.bfloat16)
    head_out = jnp.einsum(
        "rkgt,rktd->rkgd", soft_weight, cache_values, preferred_element_type=jnp.float32
    )
    return head_out.astype(jnp.bfloat16).reshape(rows, -1)


def root_norm(arrived, norm_gain):
    square_mean = jnp.mean(arrived * arrived, axis=-1, keepdims=True)
    return (arrived * lax.rsqrt(square_mean + epsilon) * norm_gain.astype(jnp.float32)).astype(
        jnp.bfloat16
    )


def expert_ffn(normed, gate_w, up_w, down_w):
    gate_act = times_transpose(normed, gate_w)
    up_act = times_transpose(normed, up_w)
    hidden = (jax.nn.silu(gate_act) * up_act).astype(jnp.bfloat16)
    return jnp.dot(hidden, down_w, preferred_element_type=jnp.float32)


def shards(
    queries,
    cache_keys,
    cache_values,
    lengths,
    out_proj,
    residual,
    norm_gain,
    expert_ids,
    gate_weights,
    owners,
    gate_proj,
    up_proj,
    down_proj,
):
    head_out = attend(queries, cache_keys, cache_values, lengths)
    attention_part = times_transpose(lax.all_gather(head_out, "dev", axis=0, tiled=True), out_proj)
    rows_all, top_count = expert_ids.shape
    experts = owners.shape[0]
    capacity = min(rows_all, 3 * top_count * rows_all // experts)
    col_count = out_proj.shape[0]
    sending, weighting = routing_tables(expert_ids, gate_weights, owners, capacity)
    residual_wide = residual.astype(jnp.float32)
    attention_out = lax.psum(attention_part, "sec")
    hidden_in = (residual_wide + attention_out).astype(jnp.bfloat16)
    outbound = jnp.dot(sending.astype(jnp.bfloat16), hidden_in, preferred_element_type=jnp.float32)
    outbound = outbound.astype(jnp.bfloat16).reshape(experts, capacity, col_count)
    inbound = lax.all_to_all(outbound, "dev", split_axis=0, concat_axis=2, tiled=True)
    arrived = inbound[0].astype(jnp.float32)
    normed = root_norm(arrived, norm_gain)
    expert_out = expert_ffn(normed, gate_proj[0], up_proj[0], down_proj[0])
    place_weight = jnp.sum(weighting, axis=1)
    own_weight = lax.dynamic_slice_in_dim(
        place_weight, lax.axis_index("dev") * capacity, capacity, 0
    )
    weighted = (expert_out * own_weight[:, None]).astype(jnp.bfloat16)
    returned = lax.all_to_all(
        weighted.reshape(1, capacity, weighted.shape[1]),
        "dev",
        split_axis=2,
        concat_axis=0,
        tiled=True,
    )
    moe = jnp.dot(
        sending.T.astype(jnp.bfloat16),
        returned.reshape(-1, col_count),
        preferred_element_type=jnp.float32,
    )
    summed = lax.psum(moe, "sec")
    return (residual_wide + attention_out + summed).astype(jnp.bfloat16)
VMEM_LIMIT = 64 * 1024 * 1024 - 64 * 1024


def fused_kernel(
    n_dev,
    queries_hbm,
    lengths_hbm,
    residual_hbm,
    gain_hbm,
    ids_hbm,
    router_hbm,
    owners_hbm,
    keys_hbm,
    values_hbm,
    out_proj_hbm,
    gate_hbm,
    up_hbm,
    down_hbm,
    output,
    queries,
    lengths,
    residual,
    gain,
    ids,
    router,
    owners,
    keys,
    values,
    out_proj,
    rising,
    down_w,
    query_rows,
    heads_in,
    heads_wide,
    part_out,
    part_in,
    hidden_in,
    cross_out,
    cross_in,
    back_out,
    back_in,
    last_out,
    last_in,
    load_sem,
    send_sem,
    recv_sem,
    pass_sem,
    back_send_sem,
    back_recv_sem,
    pair_sem,
):
    sec = lax.axis_index("sec")
    dev = lax.axis_index("dev")
    chip, core = lax.div(dev, 2), lax.rem(dev, 2)
    chips = n_dev // 2
    rows_here, kv_heads, span, head_dim = keys.shape
    group = query_rows.shape[1] // rows_here
    rows = n_dev * rows_here
    cols = out_proj.shape[0]
    units = down_w.shape[0]
    kv_width = group * head_dim

    def flipped(k):
        bit, place = 1, 0
        while bit < chips:
            place = place + lax.rem(lax.div(chip, bit) + (k // bit) % 2, 2) * bit
            bit *= 2
        return place

    chip_of = [flipped(k) for k in range(chips)]
    twin = 2 * chip + 1 - core
    to_twin = {"dev": twin}
    across = {"sec": 1 - sec}
    same = [2 * chip_of[k] + core for k in range(chips)]
    other = [2 * chip_of[k] + 1 - core for k in range(chips)]

    pairs = (
        (queries_hbm, queries),
        (keys_hbm, keys),
        (values_hbm, values),
        (lengths_hbm, lengths),
        (out_proj_hbm, out_proj),
        (residual_hbm, residual),
        (gain_hbm, gain),
        (ids_hbm, ids),
        (router_hbm, router),
        (owners_hbm, owners),
        (gate_hbm.at[0], rising.at[pl.ds(0, units)]),
        (up_hbm.at[0], rising.at[pl.ds(units, units)]),
        (down_hbm.at[0], down_w),
    )
    loads = [
        pltpu.make_async_copy(source, target, load_sem.at[i])
        for i, (source, target) in enumerate(pairs)
    ]
    for load in loads:
        load.start()

    barrier = pltpu.get_barrier_semaphore()
    for place in [across, to_twin] + [{"dev": same[k]} for k in range(1, chips)]:
        pl.semaphore_signal(barrier, inc=1, device_id=place, device_id_type=MESH)

    def remote(source, target, sent, received, place):
        return pltpu.make_async_remote_copy(
            src_ref=source,
            dst_ref=target,
            send_sem=sent,
            recv_sem=received,
            device_id=place,
            device_id_type=MESH,
        )

    def landed(phase, buffer, index):
        remote(
            buffer.at[index], buffer.at[index], send_sem.at[phase, 0],
            recv_sem.at[phase, index], to_twin,
        ).wait_recv()

    def gather_start(phase, buffer):
        copies = []
        for k in reversed(range(chips)):
            place = {"dev": same[k]} if k else to_twin
            copies.append(
                remote(
                    buffer.at[dev], buffer.at[dev], send_sem.at[phase, k],
                    recv_sem.at[phase, dev], place,
                )
            )
            copies[-1].start()
        return copies

    def gather_pass(phase, buffer, k):
        landed(phase, buffer, same[k])
        copy = remote(
            buffer.at[same[k]], buffer.at[same[k]], pass_sem.at[phase, k],
            recv_sem.at[phase, same[k]], to_twin,
        )
        copy.start()
        return copy

    loads[0].wait()
    wide_queries = queries[...].astype(jnp.float32)
    for row in range(rows_here):
        for kv in range(kv_heads):
            for g in range(group):
                start = (kv * group + g) * head_dim
                query_rows[kv, row * group + g : row * group + g + 1, :] = wide_queries[
                    row : row + 1, start : start + head_dim
                ]
    loads[1].wait()
    loads[3].wait()
    position = lax.broadcasted_iota(jnp.int32, (group, span), 1)
    sends = []
    for kv in range(kv_heads):
        scores = []
        for row in range(rows_here):
            query = query_rows[kv, row * group : (row + 1) * group, :].astype(jnp.bfloat16)
            found = times_transpose(query, keys[row, kv]) * (1.0 / math.sqrt(head_dim))
            scores.append(jnp.where(position < lengths[row], found, -jnp.inf))
        scores = jnp.concatenate(scores, axis=0)
        raised = jnp.exp(scores - jnp.max(scores, axis=1, keepdims=True))
        probs = (raised / jnp.sum(raised, axis=1, keepdims=True)).astype(jnp.bfloat16)
        if kv == 0:
            loads[2].wait()
        for row in range(rows_here):
            found = jnp.dot(
                probs[row * group : (row + 1) * group],
                values[row, kv],
                preferred_element_type=jnp.float32,
            )
            heads_in[kv, dev, row] = found.astype(jnp.bfloat16)
        if kv == 0:
            pl.semaphore_wait(barrier, chips + 1)
        sends += gather_start(kv, heads_in.at[kv])

    for i in (5, 6, 7, 8, 9):
        loads[i].wait()
    named = jnp.int32(0)
    for e in range(owners.shape[0]):
        named = named + jnp.where(owners[e] == dev, jnp.int32(e), jnp.int32(0))
    lying = jnp.sum(jnp.where(ids[...] == named, router[...], 0.0), axis=0, keepdims=True)
    square = (rows, rows)
    diagonal = lax.broadcasted_iota(jnp.int32, square, 0) == lax.broadcasted_iota(
        jnp.int32, square, 1
    )
    weight = jnp.sum(
        jnp.where(diagonal, jnp.broadcast_to(lying, square), 0.0), axis=1, keepdims=True
    )

    for kv in range(kv_heads):
        for k in range(1, chips):
            sends.append(gather_pass(kv, heads_in.at[kv], k))
    loads[4].wait()
    part = jnp.zeros((rows, cols), jnp.float32)
    for kv in range(kv_heads):
        for k in range(chips):
            landed(kv, heads_in.at[kv], other[k])
        for d in range(n_dev):
            for row in range(rows_here):
                place = (d * rows_here + row) * group
                heads_wide[kv, place : place + group, :] = heads_in[kv, d, row].astype(
                    jnp.float32
                )
        features = jnp.concatenate(
            [heads_wide[kv, pl.ds(g, rows, stride=group), :] for g in range(group)], axis=1
        ).astype(jnp.bfloat16)
        part = part + times_transpose(
            features, out_proj[:, kv * kv_width : (kv + 1) * kv_width]
        )
    part = part.astype(jnp.bfloat16)
    part_out[...] = part
    swap = remote(part_out, part_in, pair_sem.at[0, 0], pair_sem.at[0, 1], across)
    swap.start()
    sends.append(swap)
    swap.wait_recv()
    base = residual[...].astype(jnp.float32) + (
        part.astype(jnp.float32) + part_in[...].astype(jnp.float32)
    )
    hidden_in[dev] = base.astype(jnp.bfloat16)
    sends += gather_start(kv_heads, hidden_in)

    loads[10].wait()
    loads[11].wait()
    squares = jnp.zeros((rows, cols), jnp.float32)
    raising = jnp.zeros((rows, 2 * units), jnp.float32)

    def take(index, squares, raising):
        start = pl.multiple_of(index * cols, cols)
        block = hidden_in[index].astype(jnp.float32)
        scaled = (block * gain[pl.ds(start, cols)].astype(jnp.float32).reshape(1, cols)).astype(jnp.bfloat16)
        return (
            squares + block * block,
            raising + times_transpose(scaled, rising[:, pl.ds(start, cols)]),
        )

    squares, raising = take(dev, squares, raising)
    for k in range(1, chips):
        sends.append(gather_pass(kv_heads, hidden_in, k))
        landed(kv_heads, hidden_in, other[k - 1])
        squares, raising = take(same[k], squares, raising)
        squares, raising = take(other[k - 1], squares, raising)
    landed(kv_heads, hidden_in, other[chips - 1])
    squares, raising = take(other[chips - 1], squares, raising)
    square_mean = jnp.sum(squares, axis=1, keepdims=True) / (n_dev * cols)
    raising = raising * lax.rsqrt(square_mean + epsilon)
    gate_act, up_act = raising[:, :units], raising[:, units:]
    act = (gate_act * (1.0 / (1.0 + jnp.exp(-gate_act))) * up_act).astype(jnp.bfloat16)

    def lowered(index):
        start = pl.multiple_of(index * cols, cols)
        made = jnp.dot(act, down_w[:, pl.ds(start, cols)], preferred_element_type=jnp.float32)
        return made * weight

    loads[12].wait()
    halves = (range(chips - 1, chips // 2 - 1, -1), range(chips // 2 - 1, -1, -1))
    crossing = {}
    for half in halves:
        for k in half:
            cross_out[k] = lowered(other[k]).astype(jnp.bfloat16)
        for k in half:
            crossing[k] = remote(
                cross_out.at[k], cross_in.at[k], back_send_sem.at[0, k],
                back_recv_sem.at[0, k], to_twin,
            )
            crossing[k].start()
            sends.append(crossing[k])
    backs = {}
    for half in halves:
        made = {k: lowered(same[k]) for k in half}
        for k in half:
            crossing[k].wait_recv()
        for k in half:
            made[k] = made[k] + cross_in[k].astype(jnp.float32)
            if k:
                back_out[k] = made[k].astype(jnp.bfloat16)
        for k in half:
            if k == 0:
                continue
            backs[k] = remote(
                back_out.at[k], back_in.at[k], back_send_sem.at[1, k],
                back_recv_sem.at[1, k], {"dev": same[k]},
            )
            backs[k].start()
    moe = made[0]
    for copy in sends:
        copy.wait_send()
    for k in range(1, chips):
        backs[k].wait_recv()
        moe = moe + back_in[k].astype(jnp.float32)
    moe = moe.astype(jnp.bfloat16)
    last_out[...] = moe
    last = remote(last_out, last_in, pair_sem.at[1, 0], pair_sem.at[1, 1], across)
    last.start()
    for k in range(1, chips):
        backs[k].wait_send()
    last.wait_send()
    last.wait_recv()
    output[...] = (
        base + (moe.astype(jnp.float32) + last_in[...].astype(jnp.float32))
    ).astype(jnp.bfloat16)


def fused(
    n_dev,
    queries,
    cache_keys,
    cache_values,
    lengths,
    out_proj,
    residual,
    norm_gain,
    expert_ids,
    gate_weights,
    owners,
    gate_proj,
    up_proj,
    down_proj,
):
    rows_here, kv_heads, span, head_dim = cache_keys.shape
    cols = out_proj.shape[0]
    rows, width = residual.shape[0], norm_gain.shape[0]
    group = queries.shape[1] // (kv_heads * head_dim)
    units = gate_proj.shape[1]
    chips = n_dev // 2
    whole = pl.BlockSpec(memory_space=pltpu.HBM)
    wide, narrow = jnp.float32, jnp.bfloat16
    gain = norm_gain
    return pl.pallas_call(
        functools.partial(fused_kernel, n_dev),
        out_shape=jax.ShapeDtypeStruct((rows, cols), narrow),
        in_specs=[whole] * 13,
        out_specs=pl.BlockSpec(memory_space=pltpu.VMEM),
        scratch_shapes=[
            pltpu.VMEM(queries.shape, narrow),
            pltpu.SMEM(lengths.shape, jnp.int32),
            pltpu.VMEM(residual.shape, narrow),
            pltpu.VMEM(gain.shape, narrow),
            pltpu.VMEM(expert_ids.shape[::-1], jnp.int32),
            pltpu.VMEM(gate_weights.shape[::-1], wide),
            pltpu.SMEM(owners.shape, jnp.int32),
            pltpu.VMEM(cache_keys.shape, narrow),
            pltpu.VMEM(cache_values.shape, narrow),
            pltpu.VMEM(out_proj.shape, narrow),
            pltpu.VMEM((2 * units, width), narrow),
            pltpu.VMEM((units, width), narrow),
            pltpu.VMEM((kv_heads, rows_here * group, head_dim), wide),
            pltpu.VMEM((kv_heads, n_dev, rows_here, group, head_dim), narrow),
            pltpu.VMEM((kv_heads, rows * group, head_dim), wide),
            pltpu.VMEM((rows, cols), narrow),
            pltpu.VMEM((rows, cols), narrow),
            pltpu.VMEM((n_dev, rows, cols), narrow),
            pltpu.VMEM((chips, rows, cols), narrow),
            pltpu.VMEM((chips, rows, cols), narrow),
            pltpu.VMEM((chips, rows, cols), narrow),
            pltpu.VMEM((chips, rows, cols), narrow),
            pltpu.VMEM((rows, cols), narrow),
            pltpu.VMEM((rows, cols), narrow),
            pltpu.SemaphoreType.DMA((13,)),
            pltpu.SemaphoreType.DMA((kv_heads + 1, chips)),
            pltpu.SemaphoreType.DMA((kv_heads + 1, n_dev)),
            pltpu.SemaphoreType.DMA((kv_heads + 1, chips)),
            pltpu.SemaphoreType.DMA((2, chips)),
            pltpu.SemaphoreType.DMA((2, chips)),
            pltpu.SemaphoreType.DMA((2, 2)),
        ],
        compiler_params=pltpu.CompilerParams(
            collective_id=0, has_side_effects=True, vmem_limit_bytes=VMEM_LIMIT
        ),
        cost_estimate=pl.CostEstimate(
            flops=2 * rows * width * (width + 3 * units),
            bytes_accessed=2 * width * (width + 3 * units),
            transcendentals=0,
        ),
    )(
        queries,
        lengths,
        residual,
        gain,
        expert_ids.T,
        gate_weights.T,
        owners,
        cache_keys,
        cache_values,
        out_proj,
        gate_proj,
        up_proj,
        down_proj,
    )


def tiles_whole(mesh, operands):
    queries, cache_keys, _, _, out_proj, residual = operands[:6]
    owners, gate_proj = operands[9], operands[10]
    group = queries.shape[1] // (cache_keys.shape[1] * cache_keys.shape[3])
    return (
        mesh.shape["sec"] == 2
        and mesh.shape["dev"] in (4, 8, 16)
        and owners.shape[0] == mesh.shape["dev"]
        and gate_proj.shape[0] == 1
        and group % 16 == 0
        and cache_keys.shape[3] % 128 == 0
        and cache_keys.shape[2] % 128 == 0
        and residual.shape[0] % 16 == 0
        and out_proj.shape[0] % 128 == 0
        and gate_proj.shape[1] % 128 == 0
    )


def solution(mesh):
    in_specs = (
        P("dev", "sec"),
        P("dev", "sec", None, None),
        P("dev", "sec", None, None),
        P("dev"),
        P("dev", "sec"),
        P(None, "dev"),
        P(),
        P(),
        P(),
        P(),
        P("dev", "sec", None),
        P("dev", "sec", None),
        P("dev", "sec", None),
    )
    out_specs = P(None, "dev")

    def chosen(*operands):
        if tiles_whole(mesh, operands):
            return fused(mesh.shape["dev"], *operands)
        return shards(*operands)

    return jax.shard_map(chosen, mesh=mesh, in_specs=in_specs, out_specs=out_specs, check_vma=False)
```

```python
import functools
import math

import jax
import jax.numpy as jnp
from jax import lax
from jax.experimental import pallas as pl
from jax.experimental.pallas import tpu as pltpu
from jax.sharding import PartitionSpec as P

epsilon = 1e-05
MESH = pl.DeviceIdType.MESH


def slot_targets(expert_ids, owners, capacity):
    experts = owners.shape[0]
    flat_ids = expert_ids.reshape(-1)
    one_hot = (flat_ids[:, None] == jnp.arange(experts, dtype=jnp.int32)[None, :]).astype(jnp.int32)
    before = jnp.cumsum(one_hot, axis=0) - one_hot
    position = jnp.sum(before * one_hot, axis=1)
    holder = jnp.sum(one_hot * owners[None, :], axis=1)
    return (holder * capacity + position).reshape(expert_ids.shape)


def routing_tables(expert_ids, gate_weights, owners, capacity):
    target = slot_targets(expert_ids, owners, capacity)
    places = jnp.arange(owners.shape[0] * capacity, dtype=jnp.int32)
    matched = target[None, :, :] == places[:, None, None]
    sending = jnp.any(matched, axis=2)
    weighting = jnp.sum(
        jnp.where(matched, gate_weights[None, :, :], jnp.zeros_like(gate_weights)[None, :, :]),
        axis=2,
    )
    return (sending, weighting)


def times_transpose(left, right):
    return lax.dot_general(
        left, right, (((1,), (1,)), ((), ())), preferred_element_type=jnp.float32
    )


def attend(queries, cache_keys, cache_values, lengths):
    rows, kv_heads, key_span, head_dim = cache_keys.shape
    group_size = queries.shape[1] // (kv_heads * head_dim)
    grouped = queries.reshape(rows, kv_heads, group_size, head_dim)
    scores = jnp.einsum(
        "rkgd,rktd->rkgt", grouped, cache_keys, preferred_element_type=jnp.float32
    ) / math.sqrt(head_dim)
    live_mask = (
        jnp.arange(key_span, dtype=jnp.int32)[None, None, None, :] < lengths[:, None, None, None]
    )
    scores = jnp.where(live_mask, scores, -jnp.inf)
    row_top = jnp.max(scores, axis=-1, keepdims=True)
    raised = jnp.exp(scores - row_top)
    soft_weight = (raised / jnp.sum(raised, axis=-1, keepdims=True)).astype(jnp.bfloat16)
    head_out = jnp.einsum(
        "rkgt,rktd->rkgd", soft_weight, cache_values, preferred_element_type=jnp.float32
    )
    return head_out.astype(jnp.bfloat16).reshape(rows, -1)


def root_norm(arrived, norm_gain):
    square_mean = jnp.mean(arrived * arrived, axis=-1, keepdims=True)
    return (arrived * lax.rsqrt(square_mean + epsilon) * norm_gain.astype(jnp.float32)).astype(
        jnp.bfloat16
    )


def expert_ffn(normed, gate_w, up_w, down_w):
    gate_act = times_transpose(normed, gate_w)
    up_act = times_transpose(normed, up_w)
    hidden = (jax.nn.silu(gate_act) * up_act).astype(jnp.bfloat16)
    return jnp.dot(hidden, down_w, preferred_element_type=jnp.float32)


def shards(
    queries,
    cache_keys,
    cache_values,
    lengths,
    out_proj,
    residual,
    norm_gain,
    expert_ids,
    gate_weights,
    owners,
    gate_proj,
    up_proj,
    down_proj,
):
    head_out = attend(queries, cache_keys, cache_values, lengths)
    attention_part = times_transpose(lax.all_gather(head_out, "dev", axis=0, tiled=True), out_proj)
    rows_all, top_count = expert_ids.shape
    experts = owners.shape[0]
    capacity = min(rows_all, 3 * top_count * rows_all // experts)
    col_count = out_proj.shape[0]
    sending, weighting = routing_tables(expert_ids, gate_weights, owners, capacity)
    residual_wide = residual.astype(jnp.float32)
    attention_out = lax.psum(attention_part, "sec")
    hidden_in = (residual_wide + attention_out).astype(jnp.bfloat16)
    outbound = jnp.dot(sending.astype(jnp.bfloat16), hidden_in, preferred_element_type=jnp.float32)
    outbound = outbound.astype(jnp.bfloat16).reshape(experts, capacity, col_count)
    inbound = lax.all_to_all(outbound, "dev", split_axis=0, concat_axis=2, tiled=True)
    arrived = inbound[0].astype(jnp.float32)
    normed = root_norm(arrived, norm_gain)
    expert_out = expert_ffn(normed, gate_proj[0], up_proj[0], down_proj[0])
    place_weight = jnp.sum(weighting, axis=1)
    own_weight = lax.dynamic_slice_in_dim(
        place_weight, lax.axis_index("dev") * capacity, capacity, 0
    )
    weighted = (expert_out * own_weight[:, None]).astype(jnp.bfloat16)
    returned = lax.all_to_all(
        weighted.reshape(1, capacity, weighted.shape[1]),
        "dev",
        split_axis=2,
        concat_axis=0,
        tiled=True,
    )
    moe = jnp.dot(
        sending.T.astype(jnp.bfloat16),
        returned.reshape(-1, col_count),
        preferred_element_type=jnp.float32,
    )
    summed = lax.psum(moe, "sec")
    return (residual_wide + attention_out + summed).astype(jnp.bfloat16)
VMEM_LIMIT = 64 * 1024 * 1024 - 64 * 1024


def fused_kernel(
    n_dev,
    queries_hbm,
    lengths_hbm,
    residual_hbm,
    gain_hbm,
    ids_hbm,
    router_hbm,
    owners_hbm,
    keys_hbm,
    values_hbm,
    out_proj_hbm,
    gate_hbm,
    up_hbm,
    down_hbm,
    output,
    queries,
    lengths,
    residual,
    gain,
    ids,
    router,
    owners,
    keys,
    values,
    out_proj,
    rising,
    down_w,
    query_rows,
    heads_in,
    heads_wide,
    part_sum,
    part_out,
    part_in,
    hidden_in,
    cross_out,
    cross_in,
    back_out,
    back_in,
    last_out,
    last_in,
    load_sem,
    send_sem,
    recv_sem,
    pass_sem,
    pair_recv_sem,
    back_send_sem,
    back_recv_sem,
    pair_sem,
):
    sec = lax.axis_index("sec")
    dev = lax.axis_index("dev")
    chip, core = lax.div(dev, 2), lax.rem(dev, 2)
    chips = n_dev // 2
    rows_here, kv_heads, span, head_dim = keys.shape
    group = query_rows.shape[1] // rows_here
    rows = n_dev * rows_here
    cols = out_proj.shape[0]
    units = down_w.shape[0]
    kv_width = group * head_dim

    def flipped(place, k, amount):
        bit, result = 1, 0
        while bit < amount:
            result = result + lax.rem(lax.div(place, bit) + k // bit, 2) * bit
            bit *= 2
        return result

    def chip_of(k):
        return flipped(chip, k, chips)

    def pair_of(p):
        return pl.ds(2 * flipped(lax.div(chip, 2), p, chips // 2), 2)

    to_twin = {"dev": 2 * chip + 1 - core}
    across = {"sec": 1 - sec}

    pairs = (
        (queries_hbm, queries),
        (keys_hbm, keys),
        (values_hbm, values),
        (lengths_hbm, lengths),
        (out_proj_hbm, out_proj),
        (residual_hbm, residual),
        (gain_hbm, gain),
        (ids_hbm, ids),
        (router_hbm, router),
        (owners_hbm, owners),
        (gate_hbm.at[0], rising.at[pl.ds(0, units)]),
        (up_hbm.at[0], rising.at[pl.ds(units, units)]),
        (down_hbm.at[0], down_w),
    )
    loads = [
        pltpu.make_async_copy(source, target, load_sem.at[i])
        for i, (source, target) in enumerate(pairs)
    ]
    for load in loads:
        load.start()

    barrier = pltpu.get_barrier_semaphore()
    for place in (across, to_twin):
        pl.semaphore_signal(barrier, inc=1, device_id=place, device_id_type=MESH)

    @pl.loop(1, chips)
    def _(k):
        place = {"dev": 2 * chip_of(k) + core}
        pl.semaphore_signal(barrier, inc=1, device_id=place, device_id_type=MESH)

    def remote(source, target, sent, received, place):
        return pltpu.make_async_remote_copy(
            src_ref=source,
            dst_ref=target,
            send_sem=sent,
            recv_sem=received,
            device_id=place,
            device_id_type=MESH,
        )

    def sending(phase, buffer, k):
        own = buffer.at[core, chip]
        return remote(
            own, own, send_sem.at[phase, k], recv_sem.at[phase, chip],
            {"dev": 2 * chip_of(k) + core},
        )

    def gather_start(phase, buffer):
        @pl.loop(1, chips)
        def _(step):
            sending(phase, buffer, chips - step).start()

    def passing(phase, buffer, p):
        pair = buffer.at[core, pair_of(p)]
        return remote(pair, pair, pass_sem.at[phase, p], pair_recv_sem.at[phase, p], to_twin)

    def arriving(phase, buffer, k):
        block = buffer.at[core, chip_of(k)]
        remote(
            block, block, send_sem.at[phase, 0], recv_sem.at[phase, chip_of(k)], to_twin
        ).wait_recv()

    def gather_pass(phase, buffer, p):
        for k in (2 * p, 2 * p + 1):
            if not isinstance(k, int) or k:
                arriving(phase, buffer, k)
        passing(phase, buffer, p).start()

    def landed(phase, buffer, p):
        pair = buffer.at[1 - core, pair_of(p)]
        remote(
            pair, pair, pass_sem.at[phase, p], pair_recv_sem.at[phase, p], to_twin
        ).wait_recv()

    def gather_sent(phase, buffer):
        @pl.loop(1, chips)
        def _(k):
            sending(phase, buffer, k).wait_send()

        @pl.loop(0, chips // 2)
        def _(p):
            passing(phase, buffer, p).wait_send()

    loads[0].wait()
    wide_queries = queries[...].astype(jnp.float32)
    for row in range(rows_here):
        for kv in range(kv_heads):
            for g in range(group):
                start = (kv * group + g) * head_dim
                query_rows[kv, row * group + g : row * group + g + 1, :] = wide_queries[
                    row : row + 1, start : start + head_dim
                ]
    loads[1].wait()
    loads[3].wait()
    loads[2].wait()
    pl.semaphore_wait(barrier, chips + 1)
    position = lax.broadcasted_iota(jnp.int32, (group, span), 1)

    @pl.loop(0, kv_heads)
    def _(kv):
        scores = []
        for row in range(rows_here):
            query = query_rows[kv, row * group : (row + 1) * group, :].astype(jnp.bfloat16)
            found = times_transpose(query, keys[row, kv]) * (1.0 / math.sqrt(head_dim))
            scores.append(jnp.where(position < lengths[row], found, -jnp.inf))
        scores = jnp.concatenate(scores, axis=0)
        raised = jnp.exp(scores - jnp.max(scores, axis=1, keepdims=True))
        probs = (raised / jnp.sum(raised, axis=1, keepdims=True)).astype(jnp.bfloat16)
        for row in range(rows_here):
            found = jnp.dot(
                probs[row * group : (row + 1) * group],
                values[row, kv],
                preferred_element_type=jnp.float32,
            )
            heads_in[kv, core, chip, row] = found.astype(jnp.bfloat16)
        gather_start(kv, heads_in.at[kv])

    for i in (5, 6, 7, 8, 9):
        loads[i].wait()
    named = jnp.int32(0)
    for e in range(owners.shape[0]):
        named = named + jnp.where(owners[e] == dev, jnp.int32(e), jnp.int32(0))
    lying = jnp.sum(jnp.where(ids[...] == named, router[...], 0.0), axis=0, keepdims=True)
    square = (rows, rows)
    diagonal = lax.broadcasted_iota(jnp.int32, square, 0) == lax.broadcasted_iota(
        jnp.int32, square, 1
    )
    weight = jnp.sum(
        jnp.where(diagonal, jnp.broadcast_to(lying, square), 0.0), axis=1, keepdims=True
    )

    @pl.loop(0, kv_heads)
    def _(kv):
        gather_pass(kv, heads_in.at[kv], 0)

        @pl.loop(1, chips // 2)
        def _(p):
            gather_pass(kv, heads_in.at[kv], p)

    loads[4].wait()
    part_sum[...] = jnp.zeros((rows, cols), jnp.float32)

    @pl.loop(0, kv_heads)
    def _(kv):
        @pl.loop(0, chips // 2)
        def _(p):
            landed(kv, heads_in.at[kv], p)

        for d in range(n_dev):
            for row in range(rows_here):
                place = (d * rows_here + row) * group
                heads_wide[place : place + group, :] = heads_in[kv, d % 2, d // 2, row].astype(
                    jnp.float32
                )
        features = jnp.concatenate(
            [heads_wide[pl.ds(g, rows, stride=group), :] for g in range(group)], axis=1
        ).astype(jnp.bfloat16)
        start = pl.multiple_of(kv * kv_width, kv_width)
        part_sum[...] += times_transpose(features, out_proj[:, pl.ds(start, kv_width)])

    part = part_sum[...].astype(jnp.bfloat16)
    part_out[...] = part
    swap = remote(part_out, part_in, pair_sem.at[0, 0], pair_sem.at[0, 1], across)
    swap.start()
    swap.wait_recv()
    base = residual[...].astype(jnp.float32) + (
        part.astype(jnp.float32) + part_in[...].astype(jnp.float32)
    )
    hidden_in[core, chip] = base.astype(jnp.bfloat16)
    gather_start(kv_heads, hidden_in)

    loads[10].wait()
    loads[11].wait()
    squares = jnp.zeros((rows, cols), jnp.float32)
    raising = jnp.zeros((rows, 2 * units), jnp.float32)

    def take(side, p, squares, raising):
        first = pair_of(p).start
        for half in range(2):
            start = pl.multiple_of((2 * (first + half) + side) * cols, cols)
            block = hidden_in[side, first + half].astype(jnp.float32)
            scale = gain[pl.ds(start, cols)].astype(jnp.float32).reshape(1, cols)
            scaled = (block * scale).astype(jnp.bfloat16)
            squares = squares + block * block
            raising = raising + times_transpose(scaled, rising[:, pl.ds(start, cols)])
        return squares, raising

    gather_pass(kv_heads, hidden_in, 0)
    squares, raising = take(core, 0, squares, raising)

    def stage(p, carried):
        gather_pass(kv_heads, hidden_in, p)
        landed(kv_heads, hidden_in, p - 1)
        return take(1 - core, p - 1, *take(core, p, *carried))

    squares, raising = lax.fori_loop(1, chips // 2, stage, (squares, raising))
    landed(kv_heads, hidden_in, chips // 2 - 1)
    squares, raising = take(1 - core, chips // 2 - 1, squares, raising)
    square_mean = jnp.sum(squares, axis=1, keepdims=True) / (n_dev * cols)
    raising = raising * lax.rsqrt(square_mean + epsilon)
    gate_act, up_act = raising[:, :units], raising[:, units:]
    act = (gate_act * (1.0 / (1.0 + jnp.exp(-gate_act))) * up_act).astype(jnp.bfloat16)

    def lowered(side, k):
        start = pl.multiple_of((2 * chip_of(k) + side) * cols, cols)
        made = jnp.dot(act, down_w[:, pl.ds(start, cols)], preferred_element_type=jnp.float32)
        return made * weight

    loads[12].wait()
    batch = chips // 2

    def crossing(h):
        part = pl.ds(h * batch, batch)
        return remote(
            cross_out.at[part], cross_in.at[part], back_send_sem.at[0, h],
            back_recv_sem.at[0, h], to_twin,
        )

    def backing(k):
        return remote(
            back_out.at[k], back_in.at[k], back_send_sem.at[1, k], back_recv_sem.at[1, k],
            {"dev": 2 * chip_of(k) + core},
        )

    @pl.loop(0, 2)
    def _(step):
        h = 1 - step
        for i in range(batch):
            k = h * batch + i
            cross_out[k] = lowered(1 - core, k).astype(jnp.bfloat16)
        crossing(h).start()

    @pl.loop(0, 2)
    def _(step):
        h = 1 - step
        made = [lowered(core, h * batch + i) for i in range(batch)]
        crossing(h).wait_recv()
        for i in range(batch):
            k = h * batch + i
            back_out[k] = (made[i] + cross_in[k].astype(jnp.float32)).astype(jnp.bfloat16)

        @pl.loop(h * batch + step, (h + 1) * batch)
        def _(k):
            backing(k).start()

    @pl.loop(0, kv_heads)
    def _(kv):
        gather_sent(kv, heads_in.at[kv])

    gather_sent(kv_heads, hidden_in)
    swap.wait_send()

    @pl.loop(0, 2)
    def _(h):
        crossing(h).wait_send()

    def collect(k, moe):
        backing(k).wait_recv()
        return moe + back_in[k].astype(jnp.float32)

    moe = lax.fori_loop(1, chips, collect, back_out[0].astype(jnp.float32))
    moe = moe.astype(jnp.bfloat16)
    last_out[...] = moe
    last = remote(last_out, last_in, pair_sem.at[1, 0], pair_sem.at[1, 1], across)
    last.start()

    @pl.loop(1, chips)
    def _(k):
        backing(k).wait_send()

    last.wait_send()
    last.wait_recv()
    output[...] = base + (moe.astype(jnp.float32) + last_in[...].astype(jnp.float32))


def fused(
    n_dev,
    queries,
    cache_keys,
    cache_values,
    lengths,
    out_proj,
    residual,
    norm_gain,
    expert_ids,
    gate_weights,
    owners,
    gate_proj,
    up_proj,
    down_proj,
):
    rows_here, kv_heads, span, head_dim = cache_keys.shape
    cols = out_proj.shape[0]
    rows, width = residual.shape[0], norm_gain.shape[0]
    group = queries.shape[1] // (kv_heads * head_dim)
    units = gate_proj.shape[1]
    chips = n_dev // 2
    whole = pl.BlockSpec(memory_space=pltpu.HBM)
    wide, narrow = jnp.float32, jnp.bfloat16
    gain = norm_gain
    return pl.pallas_call(
        functools.partial(fused_kernel, n_dev),
        out_shape=jax.ShapeDtypeStruct((rows, cols), wide),
        in_specs=[whole] * 13,
        out_specs=pl.BlockSpec(memory_space=pltpu.VMEM),
        scratch_shapes=[
            pltpu.VMEM(queries.shape, narrow),
            pltpu.SMEM(lengths.shape, jnp.int32),
            pltpu.VMEM(residual.shape, narrow),
            pltpu.VMEM(gain.shape, narrow),
            pltpu.VMEM(expert_ids.shape[::-1], jnp.int32),
            pltpu.VMEM(gate_weights.shape[::-1], wide),
            pltpu.SMEM(owners.shape, jnp.int32),
            pltpu.VMEM(cache_keys.shape, narrow),
            pltpu.VMEM(cache_values.shape, narrow),
            pltpu.VMEM(out_proj.shape, narrow),
            pltpu.VMEM((2 * units, width), narrow),
            pltpu.VMEM((units, width), narrow),
            pltpu.VMEM((kv_heads, rows_here * group, head_dim), wide),
            pltpu.VMEM((kv_heads, 2, chips, rows_here, group, head_dim), narrow),
            pltpu.VMEM((rows * group, head_dim), wide),
            pltpu.VMEM((rows, cols), wide),
            pltpu.VMEM((rows, cols), narrow),
            pltpu.VMEM((rows, cols), narrow),
            pltpu.VMEM((2, chips, rows, cols), narrow),
            pltpu.VMEM((chips, rows, cols), narrow),
            pltpu.VMEM((chips, rows, cols), narrow),
            pltpu.VMEM((chips, rows, cols), narrow),
            pltpu.VMEM((chips, rows, cols), narrow),
            pltpu.VMEM((rows, cols), narrow),
            pltpu.VMEM((rows, cols), narrow),
            pltpu.SemaphoreType.DMA((13,)),
            pltpu.SemaphoreType.DMA((kv_heads + 1, chips)),
            pltpu.SemaphoreType.DMA((kv_heads + 1, chips)),
            pltpu.SemaphoreType.DMA((kv_heads + 1, chips // 2)),
            pltpu.SemaphoreType.DMA((kv_heads + 1, chips // 2)),
            pltpu.SemaphoreType.DMA((2, chips)),
            pltpu.SemaphoreType.DMA((2, chips)),
            pltpu.SemaphoreType.DMA((2, 2)),
        ],
        compiler_params=pltpu.CompilerParams(
            collective_id=0, has_side_effects=True, vmem_limit_bytes=VMEM_LIMIT
        ),
        cost_estimate=pl.CostEstimate(
            flops=2 * rows * width * (width + 3 * units),
            bytes_accessed=2 * width * (width + 3 * units),
            transcendentals=0,
        ),
    )(
        queries,
        lengths,
        residual,
        gain,
        expert_ids.T,
        gate_weights.T,
        owners,
        cache_keys,
        cache_values,
        out_proj,
        gate_proj,
        up_proj,
        down_proj,
    ).astype(narrow)


def tiles_whole(mesh, operands):
    queries, cache_keys, _, _, out_proj, residual = operands[:6]
    owners, gate_proj = operands[9], operands[10]
    group = queries.shape[1] // (cache_keys.shape[1] * cache_keys.shape[3])
    return (
        mesh.shape["sec"] == 2
        and mesh.shape["dev"] in (4, 8, 16)
        and owners.shape[0] == mesh.shape["dev"]
        and gate_proj.shape[0] == 1
        and group % 16 == 0
        and cache_keys.shape[3] % 128 == 0
        and cache_keys.shape[2] % 128 == 0
        and residual.shape[0] % 16 == 0
        and out_proj.shape[0] % 128 == 0
        and gate_proj.shape[1] % 128 == 0
    )


def solution(mesh):
    in_specs = (
        P("dev", "sec"),
        P("dev", "sec", None, None),
        P("dev", "sec", None, None),
        P("dev"),
        P("dev", "sec"),
        P(None, "dev"),
        P(),
        P(),
        P(),
        P(),
        P("dev", "sec", None),
        P("dev", "sec", None),
        P("dev", "sec", None),
    )
    out_specs = P(None, "dev")

    def chosen(*operands):
        if tiles_whole(mesh, operands):
            return fused(mesh.shape["dev"], *operands)
        return shards(*operands)

    return jax.shard_map(chosen, mesh=mesh, in_specs=in_specs, out_specs=out_specs, check_vma=False)
```

```python
import functools
import math

import jax
import jax.numpy as jnp
from jax import lax
from jax.experimental import pallas as pl
from jax.experimental.pallas import tpu as pltpu
from jax.sharding import PartitionSpec as P

epsilon = 1e-05
MESH = pl.DeviceIdType.MESH


def slot_targets(expert_ids, owners, capacity):
    experts = owners.shape[0]
    flat_ids = expert_ids.reshape(-1)
    one_hot = (flat_ids[:, None] == jnp.arange(experts, dtype=jnp.int32)[None, :]).astype(jnp.int32)
    before = jnp.cumsum(one_hot, axis=0) - one_hot
    position = jnp.sum(before * one_hot, axis=1)
    holder = jnp.sum(one_hot * owners[None, :], axis=1)
    return (holder * capacity + position).reshape(expert_ids.shape)


def routing_tables(expert_ids, gate_weights, owners, capacity):
    target = slot_targets(expert_ids, owners, capacity)
    places = jnp.arange(owners.shape[0] * capacity, dtype=jnp.int32)
    matched = target[None, :, :] == places[:, None, None]
    sending = jnp.any(matched, axis=2)
    weighting = jnp.sum(
        jnp.where(matched, gate_weights[None, :, :], jnp.zeros_like(gate_weights)[None, :, :]),
        axis=2,
    )
    return (sending, weighting)


def times_transpose(left, right):
    return lax.dot_general(
        left, right, (((1,), (1,)), ((), ())), preferred_element_type=jnp.float32
    )


def attend(queries, cache_keys, cache_values, lengths):
    rows, kv_heads, key_span, head_dim = cache_keys.shape
    group_size = queries.shape[1] // (kv_heads * head_dim)
    grouped = queries.reshape(rows, kv_heads, group_size, head_dim)
    scores = jnp.einsum(
        "rkgd,rktd->rkgt", grouped, cache_keys, preferred_element_type=jnp.float32
    ) / math.sqrt(head_dim)
    live_mask = (
        jnp.arange(key_span, dtype=jnp.int32)[None, None, None, :] < lengths[:, None, None, None]
    )
    scores = jnp.where(live_mask, scores, -jnp.inf)
    row_top = jnp.max(scores, axis=-1, keepdims=True)
    raised = jnp.exp(scores - row_top)
    soft_weight = (raised / jnp.sum(raised, axis=-1, keepdims=True)).astype(jnp.bfloat16)
    head_out = jnp.einsum(
        "rkgt,rktd->rkgd", soft_weight, cache_values, preferred_element_type=jnp.float32
    )
    return head_out.astype(jnp.bfloat16).reshape(rows, -1)


def root_norm(arrived, norm_gain):
    square_mean = jnp.mean(arrived * arrived, axis=-1, keepdims=True)
    return (arrived * lax.rsqrt(square_mean + epsilon) * norm_gain.astype(jnp.float32)).astype(
        jnp.bfloat16
    )


def expert_ffn(normed, gate_w, up_w, down_w):
    gate_act = times_transpose(normed, gate_w)
    up_act = times_transpose(normed, up_w)
    hidden = (jax.nn.silu(gate_act) * up_act).astype(jnp.bfloat16)
    return jnp.dot(hidden, down_w, preferred_element_type=jnp.float32)


def shards(
    queries,
    cache_keys,
    cache_values,
    lengths,
    out_proj,
    residual,
    norm_gain,
    expert_ids,
    gate_weights,
    owners,
    gate_proj,
    up_proj,
    down_proj,
):
    head_out = attend(queries, cache_keys, cache_values, lengths)
    attention_part = times_transpose(lax.all_gather(head_out, "dev", axis=0, tiled=True), out_proj)
    rows_all, top_count = expert_ids.shape
    experts = owners.shape[0]
    capacity = min(rows_all, 3 * top_count * rows_all // experts)
    col_count = out_proj.shape[0]
    sending, weighting = routing_tables(expert_ids, gate_weights, owners, capacity)
    residual_wide = residual.astype(jnp.float32)
    attention_out = lax.psum(attention_part, "sec")
    hidden_in = (residual_wide + attention_out).astype(jnp.bfloat16)
    outbound = jnp.dot(sending.astype(jnp.bfloat16), hidden_in, preferred_element_type=jnp.float32)
    outbound = outbound.astype(jnp.bfloat16).reshape(experts, capacity, col_count)
    inbound = lax.all_to_all(outbound, "dev", split_axis=0, concat_axis=2, tiled=True)
    arrived = inbound[0].astype(jnp.float32)
    normed = root_norm(arrived, norm_gain)
    expert_out = expert_ffn(normed, gate_proj[0], up_proj[0], down_proj[0])
    place_weight = jnp.sum(weighting, axis=1)
    own_weight = lax.dynamic_slice_in_dim(
        place_weight, lax.axis_index("dev") * capacity, capacity, 0
    )
    weighted = (expert_out * own_weight[:, None]).astype(jnp.bfloat16)
    returned = lax.all_to_all(
        weighted.reshape(1, capacity, weighted.shape[1]),
        "dev",
        split_axis=2,
        concat_axis=0,
        tiled=True,
    )
    moe = jnp.dot(
        sending.T.astype(jnp.bfloat16),
        returned.reshape(-1, col_count),
        preferred_element_type=jnp.float32,
    )
    summed = lax.psum(moe, "sec")
    return (residual_wide + attention_out + summed).astype(jnp.bfloat16)
VMEM_LIMIT = 32 * 1024 * 1024


def fused_kernel(
    n_dev,
    queries_hbm,
    lengths_hbm,
    residual_hbm,
    gain_hbm,
    ids_hbm,
    router_hbm,
    owners_hbm,
    keys_hbm,
    values_hbm,
    out_proj_hbm,
    gate_hbm,
    up_hbm,
    down_hbm,
    output,
    queries,
    lengths,
    residual,
    gain,
    ids,
    router,
    owners,
    keys,
    values,
    out_proj,
    rising,
    down_w,
    query_rows,
    heads_in,
    heads_wide,
    part_sum,
    part_out,
    part_in,
    hidden_in,
    cross_out,
    cross_in,
    back_out,
    back_in,
    last_out,
    last_in,
    load_sem,
    send_sem,
    recv_sem,
    pass_sem,
    pair_recv_sem,
    back_send_sem,
    back_recv_sem,
    pair_sem,
):
    sec = lax.axis_index("sec")
    dev = lax.axis_index("dev")
    chip, core = lax.div(dev, 2), lax.rem(dev, 2)
    chips = n_dev // 2
    rows_here, kv_heads, span, head_dim = keys.shape
    group = query_rows.shape[1] // rows_here
    rows = n_dev * rows_here
    cols = out_proj.shape[0]
    units = down_w.shape[0]
    kv_width = group * head_dim

    def flipped(place, k, amount):
        bit, result = 1, 0
        while bit < amount:
            result = result + lax.rem(lax.div(place, bit) + k // bit, 2) * bit
            bit *= 2
        return result

    def chip_of(k):
        return flipped(chip, k, chips)

    def pair_of(p):
        return pl.ds(2 * flipped(lax.div(chip, 2), p, chips // 2), 2)

    to_twin = {"dev": 2 * chip + 1 - core}
    across = {"sec": 1 - sec}

    pairs = (
        (queries_hbm, queries),
        (keys_hbm, keys),
        (values_hbm, values),
        (lengths_hbm, lengths),
        (out_proj_hbm, out_proj),
        (residual_hbm, residual),
        (gain_hbm, gain),
        (ids_hbm, ids),
        (router_hbm, router),
        (owners_hbm, owners),
        (gate_hbm.at[0], rising.at[pl.ds(0, units)]),
        (up_hbm.at[0], rising.at[pl.ds(units, units)]),
        (down_hbm.at[0], down_w),
    )
    loads = [
        pltpu.make_async_copy(source, target, load_sem.at[i])
        for i, (source, target) in enumerate(pairs)
    ]
    large = (4, 10, 11, 12)
    for i, load in enumerate(loads):
        if i not in large:
            load.start()

    barrier = pltpu.get_barrier_semaphore()
    for place in (across, to_twin):
        pl.semaphore_signal(barrier, inc=1, device_id=place, device_id_type=MESH)

    @pl.loop(1, chips)
    def _(k):
        place = {"dev": 2 * chip_of(k) + core}
        pl.semaphore_signal(barrier, inc=1, device_id=place, device_id_type=MESH)

    def remote(source, target, sent, received, place):
        return pltpu.make_async_remote_copy(
            src_ref=source,
            dst_ref=target,
            send_sem=sent,
            recv_sem=received,
            device_id=place,
            device_id_type=MESH,
        )

    def sending(phase, buffer, k):
        own = buffer.at[core, chip]
        return remote(
            own, own, send_sem.at[phase, k], recv_sem.at[phase, chip],
            {"dev": 2 * chip_of(k) + core},
        )

    def gather_start(phase, buffer):
        @pl.loop(1, chips)
        def _(step):
            sending(phase, buffer, chips - step).start()

    def passing(phase, buffer, p):
        pair = buffer.at[core, pair_of(p)]
        return remote(pair, pair, pass_sem.at[phase, p], pair_recv_sem.at[phase, p], to_twin)

    def arriving(phase, buffer, k):
        block = buffer.at[core, chip_of(k)]
        remote(
            block, block, send_sem.at[phase, 0], recv_sem.at[phase, chip_of(k)], to_twin
        ).wait_recv()

    def gather_pass(phase, buffer, p):
        for k in (2 * p, 2 * p + 1):
            if not isinstance(k, int) or k:
                arriving(phase, buffer, k)
        passing(phase, buffer, p).start()

    def landed(phase, buffer, p):
        pair = buffer.at[1 - core, pair_of(p)]
        remote(
            pair, pair, pass_sem.at[phase, p], pair_recv_sem.at[phase, p], to_twin
        ).wait_recv()

    def gather_sent(phase, buffer):
        @pl.loop(1, chips)
        def _(k):
            sending(phase, buffer, k).wait_send()

        @pl.loop(0, chips // 2)
        def _(p):
            passing(phase, buffer, p).wait_send()

    loads[0].wait()
    wide_queries = queries[...].astype(jnp.float32)
    for row in range(rows_here):
        for kv in range(kv_heads):
            for g in range(group):
                start = (kv * group + g) * head_dim
                query_rows[kv, row * group + g : row * group + g + 1, :] = wide_queries[
                    row : row + 1, start : start + head_dim
                ]
    loads[1].wait()
    loads[3].wait()
    loads[2].wait()
    for i in large:
        loads[i].start()
    pl.semaphore_wait(barrier, chips + 1)
    position = lax.broadcasted_iota(jnp.int32, (group, span), 1)

    @pl.loop(0, kv_heads)
    def _(kv):
        scores = []
        for row in range(rows_here):
            query = query_rows[kv, row * group : (row + 1) * group, :].astype(jnp.bfloat16)
            found = times_transpose(query, keys[row, kv]) * (1.0 / math.sqrt(head_dim))
            scores.append(jnp.where(position < lengths[row], found, -jnp.inf))
        scores = jnp.concatenate(scores, axis=0)
        raised = jnp.exp(scores - jnp.max(scores, axis=1, keepdims=True))
        probs = (raised / jnp.sum(raised, axis=1, keepdims=True)).astype(jnp.bfloat16)
        for row in range(rows_here):
            found = jnp.dot(
                probs[row * group : (row + 1) * group],
                values[row, kv],
                preferred_element_type=jnp.float32,
            )
            heads_in[kv, core, chip, row] = found.astype(jnp.bfloat16)
        gather_start(kv, heads_in.at[kv])

    for i in (5, 6, 7, 8, 9):
        loads[i].wait()
    named = jnp.int32(0)
    for e in range(owners.shape[0]):
        named = named + jnp.where(owners[e] == dev, jnp.int32(e), jnp.int32(0))
    lying = jnp.sum(jnp.where(ids[...] == named, router[...], 0.0), axis=0, keepdims=True)
    square = (rows, rows)
    diagonal = lax.broadcasted_iota(jnp.int32, square, 0) == lax.broadcasted_iota(
        jnp.int32, square, 1
    )
    weight = jnp.sum(
        jnp.where(diagonal, jnp.broadcast_to(lying, square), 0.0), axis=1, keepdims=True
    )

    @pl.loop(0, kv_heads)
    def _(kv):
        gather_pass(kv, heads_in.at[kv], 0)

        @pl.loop(1, chips // 2)
        def _(p):
            gather_pass(kv, heads_in.at[kv], p)

    loads[4].wait()
    part_sum[...] = jnp.zeros((rows, cols), jnp.float32)

    @pl.loop(0, kv_heads)
    def _(kv):
        @pl.loop(0, chips // 2)
        def _(p):
            landed(kv, heads_in.at[kv], p)

        for d in range(n_dev):
            for row in range(rows_here):
                place = (d * rows_here + row) * group
                heads_wide[place : place + group, :] = heads_in[kv, d % 2, d // 2, row].astype(
                    jnp.float32
                )
        features = jnp.concatenate(
            [heads_wide[pl.ds(g, rows, stride=group), :] for g in range(group)], axis=1
        ).astype(jnp.bfloat16)
        start = pl.multiple_of(kv * kv_width, kv_width)
        part_sum[...] += times_transpose(features, out_proj[:, pl.ds(start, kv_width)])

    part = part_sum[...].astype(jnp.bfloat16)
    part_out[...] = part
    swap = remote(part_out, part_in, pair_sem.at[0, 0], pair_sem.at[0, 1], across)
    swap.start()
    swap.wait_recv()
    base = residual[...].astype(jnp.float32) + (
        part.astype(jnp.float32) + part_in[...].astype(jnp.float32)
    )
    hidden_in[core, chip] = base.astype(jnp.bfloat16)
    gather_start(kv_heads, hidden_in)

    loads[10].wait()
    loads[11].wait()
    squares = jnp.zeros((rows, cols), jnp.float32)
    raising = jnp.zeros((rows, 2 * units), jnp.float32)

    def take(side, p, squares, raising):
        first = pair_of(p).start
        for half in range(2):
            start = pl.multiple_of((2 * (first + half) + side) * cols, cols)
            block = hidden_in[side, first + half].astype(jnp.float32)
            scale = gain[pl.ds(start, cols)].astype(jnp.float32).reshape(1, cols)
            scaled = (block * scale).astype(jnp.bfloat16)
            squares = squares + block * block
            raising = raising + times_transpose(scaled, rising[:, pl.ds(start, cols)])
        return squares, raising

    gather_pass(kv_heads, hidden_in, 0)
    squares, raising = take(core, 0, squares, raising)

    def stage(p, carried):
        gather_pass(kv_heads, hidden_in, p)
        landed(kv_heads, hidden_in, p - 1)
        return take(1 - core, p - 1, *take(core, p, *carried))

    squares, raising = lax.fori_loop(1, chips // 2, stage, (squares, raising))
    landed(kv_heads, hidden_in, chips // 2 - 1)
    squares, raising = take(1 - core, chips // 2 - 1, squares, raising)
    square_mean = jnp.sum(squares, axis=1, keepdims=True) / (n_dev * cols)
    raising = raising * lax.rsqrt(square_mean + epsilon)
    gate_act, up_act = raising[:, :units], raising[:, units:]
    act = (gate_act * (1.0 / (1.0 + jnp.exp(-gate_act))) * up_act).astype(jnp.bfloat16)

    def lowered(side, k):
        start = pl.multiple_of((2 * chip_of(k) + side) * cols, cols)
        made = jnp.dot(act, down_w[:, pl.ds(start, cols)], preferred_element_type=jnp.float32)
        return made * weight

    loads[12].wait()
    batch = chips // 2

    def crossing(h):
        part = pl.ds(h * batch, batch)
        return remote(
            cross_out.at[part], cross_in.at[part], back_send_sem.at[0, h],
            back_recv_sem.at[0, h], to_twin,
        )

    def backing(k):
        return remote(
            back_out.at[k], back_in.at[k], back_send_sem.at[1, k], back_recv_sem.at[1, k],
            {"dev": 2 * chip_of(k) + core},
        )

    @pl.loop(0, 2)
    def _(step):
        h = 1 - step
        for i in range(batch):
            k = h * batch + i
            cross_out[k] = lowered(1 - core, k).astype(jnp.bfloat16)
        crossing(h).start()

    @pl.loop(0, 2)
    def _(step):
        h = 1 - step
        made = [lowered(core, h * batch + i) for i in range(batch)]
        crossing(h).wait_recv()
        for i in range(batch):
            k = h * batch + i
            back_out[k] = (made[i] + cross_in[k].astype(jnp.float32)).astype(jnp.bfloat16)

        @pl.loop(h * batch + step, (h + 1) * batch)
        def _(k):
            backing(k).start()

    @pl.loop(0, kv_heads)
    def _(kv):
        gather_sent(kv, heads_in.at[kv])

    gather_sent(kv_heads, hidden_in)
    swap.wait_send()

    @pl.loop(0, 2)
    def _(h):
        crossing(h).wait_send()

    def collect(k, moe):
        backing(k).wait_recv()
        return moe + back_in[k].astype(jnp.float32)

    moe = lax.fori_loop(1, chips, collect, back_out[0].astype(jnp.float32))
    moe = moe.astype(jnp.bfloat16)
    last_out[...] = moe
    last = remote(last_out, last_in, pair_sem.at[1, 0], pair_sem.at[1, 1], across)
    last.start()

    @pl.loop(1, chips)
    def _(k):
        backing(k).wait_send()

    last.wait_send()
    last.wait_recv()
    output[...] = (
        base + (moe.astype(jnp.float32) + last_in[...].astype(jnp.float32))
    ).astype(jnp.bfloat16)


def fused(
    n_dev,
    queries,
    cache_keys,
    cache_values,
    lengths,
    out_proj,
    residual,
    norm_gain,
    expert_ids,
    gate_weights,
    owners,
    gate_proj,
    up_proj,
    down_proj,
):
    rows_here, kv_heads, span, head_dim = cache_keys.shape
    cols = out_proj.shape[0]
    rows, width = residual.shape[0], norm_gain.shape[0]
    group = queries.shape[1] // (kv_heads * head_dim)
    units = gate_proj.shape[1]
    chips = n_dev // 2
    whole = pl.BlockSpec(memory_space=pltpu.HBM)
    wide, narrow = jnp.float32, jnp.bfloat16
    gain = norm_gain
    operands = (
        queries,
        lengths,
        residual,
        gain,
        expert_ids.T,
        gate_weights.T,
        owners,
        cache_keys,
        cache_values,
        out_proj,
        gate_proj,
        up_proj,
        down_proj,
    )
    return pl.pallas_call(
        functools.partial(fused_kernel, n_dev),
        out_shape=pltpu.VMEM((rows, cols), narrow),
        in_specs=[whole] * 13,
        out_specs=pl.BlockSpec(memory_space=pltpu.VMEM),
        scratch_shapes=[
            pltpu.VMEM(queries.shape, narrow),
            pltpu.SMEM(lengths.shape, jnp.int32),
            pltpu.VMEM(residual.shape, narrow),
            pltpu.VMEM(gain.shape, narrow),
            pltpu.VMEM(expert_ids.shape[::-1], jnp.int32),
            pltpu.VMEM(gate_weights.shape[::-1], wide),
            pltpu.SMEM(owners.shape, jnp.int32),
            pltpu.VMEM(cache_keys.shape, narrow),
            pltpu.VMEM(cache_values.shape, narrow),
            pltpu.VMEM(out_proj.shape, narrow),
            pltpu.VMEM((2 * units, width), narrow),
            pltpu.VMEM((units, width), narrow),
            pltpu.VMEM((kv_heads, rows_here * group, head_dim), wide),
            pltpu.VMEM((kv_heads, 2, chips, rows_here, group, head_dim), narrow),
            pltpu.VMEM((rows * group, head_dim), wide),
            pltpu.VMEM((rows, cols), wide),
            pltpu.VMEM((rows, cols), narrow),
            pltpu.VMEM((rows, cols), narrow),
            pltpu.VMEM((2, chips, rows, cols), narrow),
            pltpu.VMEM((chips, rows, cols), narrow),
            pltpu.VMEM((chips, rows, cols), narrow),
            pltpu.VMEM((chips, rows, cols), narrow),
            pltpu.VMEM((chips, rows, cols), narrow),
            pltpu.VMEM((rows, cols), narrow),
            pltpu.VMEM((rows, cols), narrow),
            pltpu.SemaphoreType.DMA((13,)),
            pltpu.SemaphoreType.DMA((kv_heads + 1, chips)),
            pltpu.SemaphoreType.DMA((kv_heads + 1, chips)),
            pltpu.SemaphoreType.DMA((kv_heads + 1, chips // 2)),
            pltpu.SemaphoreType.DMA((kv_heads + 1, chips // 2)),
            pltpu.SemaphoreType.DMA((2, chips)),
            pltpu.SemaphoreType.DMA((2, chips)),
            pltpu.SemaphoreType.DMA((2, 2)),
        ],
        compiler_params=pltpu.CompilerParams(
            collective_id=0, has_side_effects=True, vmem_limit_bytes=VMEM_LIMIT
        ),
        cost_estimate=pl.CostEstimate(
            flops=2 * rows * width * (width + 3 * units),
            bytes_accessed=2 * width * (width + 3 * units),
            transcendentals=0,
        ),
    )(*(pltpu.with_memory_space_constraint(operand, pltpu.HBM) for operand in operands))


def tiles_whole(mesh, operands):
    queries, cache_keys, _, _, out_proj, residual = operands[:6]
    owners, gate_proj = operands[9], operands[10]
    group = queries.shape[1] // (cache_keys.shape[1] * cache_keys.shape[3])
    return (
        mesh.shape["sec"] == 2
        and mesh.shape["dev"] in (4, 8, 16)
        and owners.shape[0] == mesh.shape["dev"]
        and gate_proj.shape[0] == 1
        and group % 16 == 0
        and cache_keys.shape[3] % 128 == 0
        and cache_keys.shape[2] % 128 == 0
        and residual.shape[0] % 16 == 0
        and out_proj.shape[0] % 128 == 0
        and gate_proj.shape[1] % 128 == 0
    )


def solution(mesh):
    in_specs = (
        P("dev", "sec"),
        P("dev", "sec", None, None),
        P("dev", "sec", None, None),
        P("dev"),
        P("dev", "sec"),
        P(None, "dev"),
        P(),
        P(),
        P(),
        P(),
        P("dev", "sec", None),
        P("dev", "sec", None),
        P("dev", "sec", None),
    )
    out_specs = P(None, "dev")

    def chosen(*operands):
        if tiles_whole(mesh, operands):
            return fused(mesh.shape["dev"], *operands)
        return shards(*operands)

    return jax.shard_map(chosen, mesh=mesh, in_specs=in_specs, out_specs=out_specs, check_vma=False)
```

```python
import functools
import math

import jax
import jax.numpy as jnp
from jax import lax
from jax.experimental import pallas as pl
from jax.experimental.pallas import tpu as pltpu
from jax.sharding import PartitionSpec as P

epsilon = 1e-05
MESH = pl.DeviceIdType.MESH


def slot_targets(expert_ids, owners, capacity):
    experts = owners.shape[0]
    flat_ids = expert_ids.reshape(-1)
    one_hot = (flat_ids[:, None] == jnp.arange(experts, dtype=jnp.int32)[None, :]).astype(jnp.int32)
    before = jnp.cumsum(one_hot, axis=0) - one_hot
    position = jnp.sum(before * one_hot, axis=1)
    holder = jnp.sum(one_hot * owners[None, :], axis=1)
    return (holder * capacity + position).reshape(expert_ids.shape)


def routing_tables(expert_ids, gate_weights, owners, capacity):
    target = slot_targets(expert_ids, owners, capacity)
    places = jnp.arange(owners.shape[0] * capacity, dtype=jnp.int32)
    matched = target[None, :, :] == places[:, None, None]
    sending = jnp.any(matched, axis=2)
    weighting = jnp.sum(
        jnp.where(matched, gate_weights[None, :, :], jnp.zeros_like(gate_weights)[None, :, :]),
        axis=2,
    )
    return (sending, weighting)


def times_transpose(left, right):
    return lax.dot_general(
        left, right, (((1,), (1,)), ((), ())), preferred_element_type=jnp.float32
    )


def attend(queries, cache_keys, cache_values, lengths):
    rows, kv_heads, key_span, head_dim = cache_keys.shape
    group_size = queries.shape[1] // (kv_heads * head_dim)
    grouped = queries.reshape(rows, kv_heads, group_size, head_dim)
    scores = jnp.einsum(
        "rkgd,rktd->rkgt", grouped, cache_keys, preferred_element_type=jnp.float32
    ) / math.sqrt(head_dim)
    live_mask = (
        jnp.arange(key_span, dtype=jnp.int32)[None, None, None, :] < lengths[:, None, None, None]
    )
    scores = jnp.where(live_mask, scores, -jnp.inf)
    row_top = jnp.max(scores, axis=-1, keepdims=True)
    raised = jnp.exp(scores - row_top)
    soft_weight = (raised / jnp.sum(raised, axis=-1, keepdims=True)).astype(jnp.bfloat16)
    head_out = jnp.einsum(
        "rkgt,rktd->rkgd", soft_weight, cache_values, preferred_element_type=jnp.float32
    )
    return head_out.astype(jnp.bfloat16).reshape(rows, -1)


def root_norm(arrived, norm_gain):
    square_mean = jnp.mean(arrived * arrived, axis=-1, keepdims=True)
    return (arrived * lax.rsqrt(square_mean + epsilon) * norm_gain.astype(jnp.float32)).astype(
        jnp.bfloat16
    )


def expert_ffn(normed, gate_w, up_w, down_w):
    gate_act = times_transpose(normed, gate_w)
    up_act = times_transpose(normed, up_w)
    hidden = (jax.nn.silu(gate_act) * up_act).astype(jnp.bfloat16)
    return jnp.dot(hidden, down_w, preferred_element_type=jnp.float32)


def shards(
    queries,
    cache_keys,
    cache_values,
    lengths,
    out_proj,
    residual,
    norm_gain,
    expert_ids,
    gate_weights,
    owners,
    gate_proj,
    up_proj,
    down_proj,
):
    head_out = attend(queries, cache_keys, cache_values, lengths)
    attention_part = times_transpose(lax.all_gather(head_out, "dev", axis=0, tiled=True), out_proj)
    rows_all, top_count = expert_ids.shape
    experts = owners.shape[0]
    capacity = min(rows_all, 3 * top_count * rows_all // experts)
    col_count = out_proj.shape[0]
    sending, weighting = routing_tables(expert_ids, gate_weights, owners, capacity)
    residual_wide = residual.astype(jnp.float32)
    attention_out = lax.psum(attention_part, "sec")
    hidden_in = (residual_wide + attention_out).astype(jnp.bfloat16)
    outbound = jnp.dot(sending.astype(jnp.bfloat16), hidden_in, preferred_element_type=jnp.float32)
    outbound = outbound.astype(jnp.bfloat16).reshape(experts, capacity, col_count)
    inbound = lax.all_to_all(outbound, "dev", split_axis=0, concat_axis=2, tiled=True)
    arrived = inbound[0].astype(jnp.float32)
    normed = root_norm(arrived, norm_gain)
    expert_out = expert_ffn(normed, gate_proj[0], up_proj[0], down_proj[0])
    place_weight = jnp.sum(weighting, axis=1)
    own_weight = lax.dynamic_slice_in_dim(
        place_weight, lax.axis_index("dev") * capacity, capacity, 0
    )
    weighted = (expert_out * own_weight[:, None]).astype(jnp.bfloat16)
    returned = lax.all_to_all(
        weighted.reshape(1, capacity, weighted.shape[1]),
        "dev",
        split_axis=2,
        concat_axis=0,
        tiled=True,
    )
    moe = jnp.dot(
        sending.T.astype(jnp.bfloat16),
        returned.reshape(-1, col_count),
        preferred_element_type=jnp.float32,
    )
    summed = lax.psum(moe, "sec")
    return (residual_wide + attention_out + summed).astype(jnp.bfloat16)
VMEM_LIMIT = 32 * 1024 * 1024


def fused_kernel(
    n_dev,
    queries_hbm,
    lengths_hbm,
    residual_hbm,
    gain_hbm,
    ids_hbm,
    router_hbm,
    owners_hbm,
    keys_hbm,
    values_hbm,
    out_proj_hbm,
    gate_hbm,
    up_hbm,
    down_hbm,
    output,
    queries,
    lengths,
    residual,
    gain,
    ids,
    router,
    owners,
    keys,
    values,
    out_proj,
    rising,
    down_w,
    query_rows,
    heads_in,
    heads_wide,
    part_sum,
    part_out,
    part_in,
    hidden_in,
    cross_out,
    cross_in,
    back_out,
    back_in,
    last_out,
    last_in,
    load_sem,
    send_sem,
    recv_sem,
    pass_sem,
    pair_recv_sem,
    back_send_sem,
    back_recv_sem,
    pair_sem,
):
    sec = lax.axis_index("sec")
    dev = lax.axis_index("dev")
    chip, core = lax.div(dev, 2), lax.rem(dev, 2)
    chips = n_dev // 2
    rows_here, kv_heads, span, head_dim = keys.shape
    group = query_rows.shape[1] // rows_here
    rows = n_dev * rows_here
    cols = out_proj.shape[0]
    units = down_w.shape[0]
    kv_width = group * head_dim

    def flipped(place, k, amount):
        bit, result = 1, 0
        while bit < amount:
            result = result + lax.rem(lax.div(place, bit) + k // bit, 2) * bit
            bit *= 2
        return result

    def chip_of(k):
        return flipped(chip, k, chips)

    def pair_of(p):
        return pl.ds(2 * flipped(lax.div(chip, 2), p, chips // 2), 2)

    to_twin = {"dev": 2 * chip + 1 - core}
    across = {"sec": 1 - sec}

    pairs = (
        (queries_hbm, queries),
        (keys_hbm, keys),
        (values_hbm, values),
        (lengths_hbm, lengths),
        (out_proj_hbm, out_proj),
        (residual_hbm, residual),
        (gain_hbm, gain),
        (ids_hbm, ids),
        (router_hbm, router),
        (owners_hbm, owners),
        (gate_hbm.at[0], rising.at[pl.ds(0, units)]),
        (up_hbm.at[0], rising.at[pl.ds(units, units)]),
        (down_hbm.at[0], down_w),
    )
    loads = [
        pltpu.make_async_copy(source, target, load_sem.at[i])
        for i, (source, target) in enumerate(pairs)
    ]
    large = (4, 10, 11, 12)
    for i, load in enumerate(loads):
        if i not in large:
            load.start()

    barrier = pltpu.get_barrier_semaphore()
    for place in (across, to_twin):
        pl.semaphore_signal(barrier, inc=1, device_id=place, device_id_type=MESH)

    @pl.loop(1, chips)
    def _(k):
        place = {"dev": 2 * chip_of(k) + core}
        pl.semaphore_signal(barrier, inc=1, device_id=place, device_id_type=MESH)

    def remote(source, target, sent, received, place):
        return pltpu.make_async_remote_copy(
            src_ref=source,
            dst_ref=target,
            send_sem=sent,
            recv_sem=received,
            device_id=place,
            device_id_type=MESH,
        )

    def sending(phase, buffer, k):
        own = buffer.at[core, chip]
        return remote(
            own, own, send_sem.at[phase, k], recv_sem.at[phase, chip],
            {"dev": 2 * chip_of(k) + core},
        )

    def gather_start(phase, buffer):
        @pl.loop(1, chips // 2)
        def _(step):
            sending(phase, buffer, chips - 2 * step).start()

        sending(phase, buffer, 1).start()

    def relaying(phase, buffer, p):
        place = chip_of(2 * p)
        block = buffer.at[core, place]
        return remote(
            block, block, send_sem.at[phase, 2 * p + 1], recv_sem.at[phase, place],
            {"dev": 2 * chip_of(1) + core},
        )

    def passing(phase, buffer, p):
        pair = buffer.at[core, pair_of(p)]
        return remote(pair, pair, pass_sem.at[phase, p], pair_recv_sem.at[phase, p], to_twin)

    def arriving(phase, buffer, k):
        block = buffer.at[core, chip_of(k)]
        remote(
            block, block, send_sem.at[phase, 0], recv_sem.at[phase, chip_of(k)], to_twin
        ).wait_recv()

    def gather_relay(phase, buffer, p):
        arriving(phase, buffer, 2 * p)
        relaying(phase, buffer, p).start()

    def gather_pass(phase, buffer, p):
        arriving(phase, buffer, 2 * p + 1)
        passing(phase, buffer, p).start()

    def landed(phase, buffer, p):
        pair = buffer.at[1 - core, pair_of(p)]
        remote(
            pair, pair, pass_sem.at[phase, p], pair_recv_sem.at[phase, p], to_twin
        ).wait_recv()

    def gather_sent(phase, buffer):
        sending(phase, buffer, 1).wait_send()

        @pl.loop(1, chips // 2)
        def _(p):
            sending(phase, buffer, 2 * p).wait_send()
            relaying(phase, buffer, p).wait_send()

        @pl.loop(0, chips // 2)
        def _(p):
            passing(phase, buffer, p).wait_send()

    loads[0].wait()
    wide_queries = queries[...].astype(jnp.float32)
    for row in range(rows_here):
        for kv in range(kv_heads):
            for g in range(group):
                start = (kv * group + g) * head_dim
                query_rows[kv, row * group + g : row * group + g + 1, :] = wide_queries[
                    row : row + 1, start : start + head_dim
                ]
    loads[1].wait()
    loads[3].wait()
    loads[2].wait()
    for i in large:
        loads[i].start()
    pl.semaphore_wait(barrier, chips + 1)
    position = lax.broadcasted_iota(jnp.int32, (group, span), 1)

    @pl.loop(0, kv_heads)
    def _(kv):
        scores = []
        for row in range(rows_here):
            query = query_rows[kv, row * group : (row + 1) * group, :].astype(jnp.bfloat16)
            found = times_transpose(query, keys[row, kv]) * (1.0 / math.sqrt(head_dim))
            scores.append(jnp.where(position < lengths[row], found, -jnp.inf))
        scores = jnp.concatenate(scores, axis=0)
        raised = jnp.exp(scores - jnp.max(scores, axis=1, keepdims=True))
        probs = (raised / jnp.sum(raised, axis=1, keepdims=True)).astype(jnp.bfloat16)
        for row in range(rows_here):
            found = jnp.dot(
                probs[row * group : (row + 1) * group],
                values[row, kv],
                preferred_element_type=jnp.float32,
            )
            heads_in[kv, core, chip, row] = found.astype(jnp.bfloat16)
        gather_start(kv, heads_in.at[kv])

    for i in (5, 6, 7, 8, 9):
        loads[i].wait()
    named = jnp.int32(0)
    for e in range(owners.shape[0]):
        named = named + jnp.where(owners[e] == dev, jnp.int32(e), jnp.int32(0))
    lying = jnp.sum(jnp.where(ids[...] == named, router[...], 0.0), axis=0, keepdims=True)
    square = (rows, rows)
    diagonal = lax.broadcasted_iota(jnp.int32, square, 0) == lax.broadcasted_iota(
        jnp.int32, square, 1
    )
    weight = jnp.sum(
        jnp.where(diagonal, jnp.broadcast_to(lying, square), 0.0), axis=1, keepdims=True
    )

    @pl.loop(0, kv_heads)
    def _(kv):
        @pl.loop(1, chips // 2)
        def _(p):
            gather_relay(kv, heads_in.at[kv], p)

    @pl.loop(0, kv_heads)
    def _(kv):
        gather_pass(kv, heads_in.at[kv], 0)

        @pl.loop(1, chips // 2)
        def _(p):
            gather_pass(kv, heads_in.at[kv], p)

    loads[4].wait()
    part_sum[...] = jnp.zeros((rows, cols), jnp.float32)

    @pl.loop(0, kv_heads)
    def _(kv):
        @pl.loop(0, chips // 2)
        def _(p):
            landed(kv, heads_in.at[kv], p)

        for d in range(n_dev):
            for row in range(rows_here):
                place = (d * rows_here + row) * group
                heads_wide[place : place + group, :] = heads_in[kv, d % 2, d // 2, row].astype(
                    jnp.float32
                )
        features = jnp.concatenate(
            [heads_wide[pl.ds(g, rows, stride=group), :] for g in range(group)], axis=1
        ).astype(jnp.bfloat16)
        start = pl.multiple_of(kv * kv_width, kv_width)
        part_sum[...] += times_transpose(features, out_proj[:, pl.ds(start, kv_width)])

    part = part_sum[...].astype(jnp.bfloat16)
    part_out[...] = part
    swap = remote(part_out, part_in, pair_sem.at[0, 0], pair_sem.at[0, 1], across)
    swap.start()
    swap.wait_recv()
    base = residual[...].astype(jnp.float32) + (
        part.astype(jnp.float32) + part_in[...].astype(jnp.float32)
    )
    hidden_in[core, chip] = base.astype(jnp.bfloat16)
    gather_start(kv_heads, hidden_in)

    loads[10].wait()
    loads[11].wait()
    squares = jnp.zeros((rows, cols), jnp.float32)
    raising = jnp.zeros((rows, 2 * units), jnp.float32)

    def take(side, p, squares, raising):
        first = pair_of(p).start
        for half in range(2):
            start = pl.multiple_of((2 * (first + half) + side) * cols, cols)
            block = hidden_in[side, first + half].astype(jnp.float32)
            scale = gain[pl.ds(start, cols)].astype(jnp.float32).reshape(1, cols)
            scaled = (block * scale).astype(jnp.bfloat16)
            squares = squares + block * block
            raising = raising + times_transpose(scaled, rising[:, pl.ds(start, cols)])
        return squares, raising

    gather_relay(kv_heads, hidden_in, 1)
    gather_pass(kv_heads, hidden_in, 0)
    squares, raising = take(core, 0, squares, raising)

    def stage(p, carried):
        @pl.when(p < chips // 2 - 1)
        def _():
            gather_relay(kv_heads, hidden_in, p + 1)

        gather_pass(kv_heads, hidden_in, p)
        landed(kv_heads, hidden_in, p - 1)
        return take(1 - core, p - 1, *take(core, p, *carried))

    squares, raising = lax.fori_loop(1, chips // 2, stage, (squares, raising))
    landed(kv_heads, hidden_in, chips // 2 - 1)
    squares, raising = take(1 - core, chips // 2 - 1, squares, raising)
    square_mean = jnp.sum(squares, axis=1, keepdims=True) / (n_dev * cols)
    raising = raising * lax.rsqrt(square_mean + epsilon)
    gate_act, up_act = raising[:, :units], raising[:, units:]
    act = (gate_act * (1.0 / (1.0 + jnp.exp(-gate_act))) * up_act).astype(jnp.bfloat16)

    def lowered(side, k):
        start = pl.multiple_of((2 * chip_of(k) + side) * cols, cols)
        made = jnp.dot(act, down_w[:, pl.ds(start, cols)], preferred_element_type=jnp.float32)
        return made * weight

    loads[12].wait()
    batch = chips // 2

    def crossing(h):
        part = pl.ds(h * batch, batch)
        return remote(
            cross_out.at[part], cross_in.at[part], back_send_sem.at[0, h],
            back_recv_sem.at[0, h], to_twin,
        )

    def backing(k):
        return remote(
            back_out.at[k], back_in.at[k], back_send_sem.at[1, k], back_recv_sem.at[1, k],
            {"dev": 2 * chip_of(k) + core},
        )

    @pl.loop(0, 2)
    def _(step):
        h = 1 - step
        for i in range(batch):
            k = h * batch + i
            cross_out[k] = lowered(1 - core, k).astype(jnp.bfloat16)
        crossing(h).start()

    @pl.loop(0, 2)
    def _(step):
        h = 1 - step
        made = [lowered(core, h * batch + i) for i in range(batch)]
        crossing(h).wait_recv()
        for i in range(batch):
            k = h * batch + i
            back_out[k] = (made[i] + cross_in[k].astype(jnp.float32)).astype(jnp.bfloat16)

        @pl.loop(h * batch + step, (h + 1) * batch)
        def _(k):
            backing(k).start()

    @pl.loop(0, kv_heads)
    def _(kv):
        gather_sent(kv, heads_in.at[kv])

    gather_sent(kv_heads, hidden_in)
    swap.wait_send()

    @pl.loop(0, 2)
    def _(h):
        crossing(h).wait_send()

    def collect(k, moe):
        backing(k).wait_recv()
        return moe + back_in[k].astype(jnp.float32)

    moe = lax.fori_loop(1, chips, collect, back_out[0].astype(jnp.float32))
    moe = moe.astype(jnp.bfloat16)
    last_out[...] = moe
    last = remote(last_out, last_in, pair_sem.at[1, 0], pair_sem.at[1, 1], across)
    last.start()

    @pl.loop(1, chips)
    def _(k):
        backing(k).wait_send()

    last.wait_send()
    last.wait_recv()
    output[...] = (
        base + (moe.astype(jnp.float32) + last_in[...].astype(jnp.float32))
    ).astype(jnp.bfloat16)


def fused(
    n_dev,
    queries,
    cache_keys,
    cache_values,
    lengths,
    out_proj,
    residual,
    norm_gain,
    expert_ids,
    gate_weights,
    owners,
    gate_proj,
    up_proj,
    down_proj,
):
    rows_here, kv_heads, span, head_dim = cache_keys.shape
    cols = out_proj.shape[0]
    rows, width = residual.shape[0], norm_gain.shape[0]
    group = queries.shape[1] // (kv_heads * head_dim)
    units = gate_proj.shape[1]
    chips = n_dev // 2
    whole = pl.BlockSpec(memory_space=pltpu.HBM)
    wide, narrow = jnp.float32, jnp.bfloat16
    gain = norm_gain
    operands = (
        queries,
        lengths,
        residual,
        gain,
        expert_ids.T,
        gate_weights.T,
        owners,
        cache_keys,
        cache_values,
        out_proj,
        gate_proj,
        up_proj,
        down_proj,
    )
    return pl.pallas_call(
        functools.partial(fused_kernel, n_dev),
        out_shape=pltpu.VMEM((rows, cols), narrow),
        in_specs=[whole] * 13,
        out_specs=pl.BlockSpec(memory_space=pltpu.VMEM),
        scratch_shapes=[
            pltpu.VMEM(queries.shape, narrow),
            pltpu.SMEM(lengths.shape, jnp.int32),
            pltpu.VMEM(residual.shape, narrow),
            pltpu.VMEM(gain.shape, narrow),
            pltpu.VMEM(expert_ids.shape[::-1], jnp.int32),
            pltpu.VMEM(gate_weights.shape[::-1], wide),
            pltpu.SMEM(owners.shape, jnp.int32),
            pltpu.VMEM(cache_keys.shape, narrow),
            pltpu.VMEM(cache_values.shape, narrow),
            pltpu.VMEM(out_proj.shape, narrow),
            pltpu.VMEM((2 * units, width), narrow),
            pltpu.VMEM((units, width), narrow),
            pltpu.VMEM((kv_heads, rows_here * group, head_dim), wide),
            pltpu.VMEM((kv_heads, 2, chips, rows_here, group, head_dim), narrow),
            pltpu.VMEM((rows * group, head_dim), wide),
            pltpu.VMEM((rows, cols), wide),
            pltpu.VMEM((rows, cols), narrow),
            pltpu.VMEM((rows, cols), narrow),
            pltpu.VMEM((2, chips, rows, cols), narrow),
            pltpu.VMEM((chips, rows, cols), narrow),
            pltpu.VMEM((chips, rows, cols), narrow),
            pltpu.VMEM((chips, rows, cols), narrow),
            pltpu.VMEM((chips, rows, cols), narrow),
            pltpu.VMEM((rows, cols), narrow),
            pltpu.VMEM((rows, cols), narrow),
            pltpu.SemaphoreType.DMA((13,)),
            pltpu.SemaphoreType.DMA((kv_heads + 1, chips)),
            pltpu.SemaphoreType.DMA((kv_heads + 1, chips)),
            pltpu.SemaphoreType.DMA((kv_heads + 1, chips // 2)),
            pltpu.SemaphoreType.DMA((kv_heads + 1, chips // 2)),
            pltpu.SemaphoreType.DMA((2, chips)),
            pltpu.SemaphoreType.DMA((2, chips)),
            pltpu.SemaphoreType.DMA((2, 2)),
        ],
        compiler_params=pltpu.CompilerParams(
            collective_id=0, has_side_effects=True, vmem_limit_bytes=VMEM_LIMIT
        ),
        cost_estimate=pl.CostEstimate(
            flops=2 * rows * width * (width + 3 * units),
            bytes_accessed=2 * width * (width + 3 * units),
            transcendentals=0,
        ),
    )(*(pltpu.with_memory_space_constraint(operand, pltpu.HBM) for operand in operands))


def tiles_whole(mesh, operands):
    queries, cache_keys, _, _, out_proj, residual = operands[:6]
    owners, gate_proj = operands[9], operands[10]
    group = queries.shape[1] // (cache_keys.shape[1] * cache_keys.shape[3])
    return (
        mesh.shape["sec"] == 2
        and mesh.shape["dev"] in (4, 8, 16)
        and owners.shape[0] == mesh.shape["dev"]
        and gate_proj.shape[0] == 1
        and group % 16 == 0
        and cache_keys.shape[3] % 128 == 0
        and cache_keys.shape[2] % 128 == 0
        and residual.shape[0] % 16 == 0
        and out_proj.shape[0] % 128 == 0
        and gate_proj.shape[1] % 128 == 0
    )


def solution(mesh):
    in_specs = (
        P("dev", "sec"),
        P("dev", "sec", None, None),
        P("dev", "sec", None, None),
        P("dev"),
        P("dev", "sec"),
        P(None, "dev"),
        P(),
        P(),
        P(),
        P(),
        P("dev", "sec", None),
        P("dev", "sec", None),
        P("dev", "sec", None),
    )
    out_specs = P(None, "dev")

    def chosen(*operands):
        if tiles_whole(mesh, operands):
            return fused(mesh.shape["dev"], *operands)
        return shards(*operands)

    return jax.shard_map(chosen, mesh=mesh, in_specs=in_specs, out_specs=out_specs, check_vma=False)
```

```python
import functools
import math

import jax
import jax.numpy as jnp
from jax import lax
from jax.experimental import pallas as pl
from jax.experimental.pallas import tpu as pltpu
from jax.sharding import PartitionSpec as P

epsilon = 1e-05
MESH = pl.DeviceIdType.MESH


def slot_targets(expert_ids, owners, capacity):
    experts = owners.shape[0]
    flat_ids = expert_ids.reshape(-1)
    one_hot = (flat_ids[:, None] == jnp.arange(experts, dtype=jnp.int32)[None, :]).astype(jnp.int32)
    before = jnp.cumsum(one_hot, axis=0) - one_hot
    position = jnp.sum(before * one_hot, axis=1)
    holder = jnp.sum(one_hot * owners[None, :], axis=1)
    return (holder * capacity + position).reshape(expert_ids.shape)


def routing_tables(expert_ids, gate_weights, owners, capacity):
    target = slot_targets(expert_ids, owners, capacity)
    places = jnp.arange(owners.shape[0] * capacity, dtype=jnp.int32)
    matched = target[None, :, :] == places[:, None, None]
    sending = jnp.any(matched, axis=2)
    weighting = jnp.sum(
        jnp.where(matched, gate_weights[None, :, :], jnp.zeros_like(gate_weights)[None, :, :]),
        axis=2,
    )
    return (sending, weighting)


def times_transpose(left, right):
    return lax.dot_general(
        left, right, (((1,), (1,)), ((), ())), preferred_element_type=jnp.float32
    )


def attend(queries, cache_keys, cache_values, lengths):
    rows, kv_heads, key_span, head_dim = cache_keys.shape
    group_size = queries.shape[1] // (kv_heads * head_dim)
    grouped = queries.reshape(rows, kv_heads, group_size, head_dim)
    scores = jnp.einsum(
        "rkgd,rktd->rkgt", grouped, cache_keys, preferred_element_type=jnp.float32
    ) / math.sqrt(head_dim)
    live_mask = (
        jnp.arange(key_span, dtype=jnp.int32)[None, None, None, :] < lengths[:, None, None, None]
    )
    scores = jnp.where(live_mask, scores, -jnp.inf)
    row_top = jnp.max(scores, axis=-1, keepdims=True)
    raised = jnp.exp(scores - row_top)
    soft_weight = (raised / jnp.sum(raised, axis=-1, keepdims=True)).astype(jnp.bfloat16)
    head_out = jnp.einsum(
        "rkgt,rktd->rkgd", soft_weight, cache_values, preferred_element_type=jnp.float32
    )
    return head_out.astype(jnp.bfloat16).reshape(rows, -1)


def root_norm(arrived, norm_gain):
    square_mean = jnp.mean(arrived * arrived, axis=-1, keepdims=True)
    return (arrived * lax.rsqrt(square_mean + epsilon) * norm_gain.astype(jnp.float32)).astype(
        jnp.bfloat16
    )


def expert_ffn(normed, gate_w, up_w, down_w):
    gate_act = times_transpose(normed, gate_w)
    up_act = times_transpose(normed, up_w)
    hidden = (jax.nn.silu(gate_act) * up_act).astype(jnp.bfloat16)
    return jnp.dot(hidden, down_w, preferred_element_type=jnp.float32)


def shards(
    queries,
    cache_keys,
    cache_values,
    lengths,
    out_proj,
    residual,
    norm_gain,
    expert_ids,
    gate_weights,
    owners,
    gate_proj,
    up_proj,
    down_proj,
):
    head_out = attend(queries, cache_keys, cache_values, lengths)
    attention_part = times_transpose(lax.all_gather(head_out, "dev", axis=0, tiled=True), out_proj)
    rows_all, top_count = expert_ids.shape
    experts = owners.shape[0]
    capacity = min(rows_all, 3 * top_count * rows_all // experts)
    col_count = out_proj.shape[0]
    sending, weighting = routing_tables(expert_ids, gate_weights, owners, capacity)
    residual_wide = residual.astype(jnp.float32)
    attention_out = lax.psum(attention_part, "sec")
    hidden_in = (residual_wide + attention_out).astype(jnp.bfloat16)
    outbound = jnp.dot(sending.astype(jnp.bfloat16), hidden_in, preferred_element_type=jnp.float32)
    outbound = outbound.astype(jnp.bfloat16).reshape(experts, capacity, col_count)
    inbound = lax.all_to_all(outbound, "dev", split_axis=0, concat_axis=2, tiled=True)
    arrived = inbound[0].astype(jnp.float32)
    normed = root_norm(arrived, norm_gain)
    expert_out = expert_ffn(normed, gate_proj[0], up_proj[0], down_proj[0])
    place_weight = jnp.sum(weighting, axis=1)
    own_weight = lax.dynamic_slice_in_dim(
        place_weight, lax.axis_index("dev") * capacity, capacity, 0
    )
    weighted = (expert_out * own_weight[:, None]).astype(jnp.bfloat16)
    returned = lax.all_to_all(
        weighted.reshape(1, capacity, weighted.shape[1]),
        "dev",
        split_axis=2,
        concat_axis=0,
        tiled=True,
    )
    moe = jnp.dot(
        sending.T.astype(jnp.bfloat16),
        returned.reshape(-1, col_count),
        preferred_element_type=jnp.float32,
    )
    summed = lax.psum(moe, "sec")
    return (residual_wide + attention_out + summed).astype(jnp.bfloat16)
VMEM_LIMIT = 32 * 1024 * 1024


def fused_kernel(
    n_dev,
    queries_hbm,
    lengths_hbm,
    residual_hbm,
    gain_hbm,
    ids_hbm,
    router_hbm,
    owners_hbm,
    keys_hbm,
    values_hbm,
    out_proj_hbm,
    gate_hbm,
    up_hbm,
    down_hbm,
    output,
    queries,
    lengths,
    residual,
    gain,
    ids,
    router,
    owners,
    keys,
    values,
    out_proj,
    rising,
    down_w,
    query_rows,
    heads_in,
    heads_wide,
    part_sum,
    part_out,
    part_in,
    hidden_in,
    cross_out,
    cross_in,
    back_out,
    back_in,
    last_out,
    last_in,
    load_sem,
    send_sem,
    recv_sem,
    back_send_sem,
    back_recv_sem,
    pair_sem,
):
    sec = lax.axis_index("sec")
    dev = lax.axis_index("dev")
    chip, core = lax.div(dev, 2), lax.rem(dev, 2)
    chips = n_dev // 2
    rows_here, kv_heads, span, head_dim = keys.shape
    group = query_rows.shape[1] // rows_here
    rows = n_dev * rows_here
    cols = out_proj.shape[0]
    units = down_w.shape[0]
    kv_width = group * head_dim

    def flipped(place, k, amount):
        bit, result = 1, 0
        while bit < amount:
            result = result + lax.rem(lax.div(place, bit) + k // bit, 2) * bit
            bit *= 2
        return result

    def chip_of(k):
        return flipped(chip, k, chips)

    def device_of(k):
        place = flipped(dev, k, n_dev)
        return lax.div(place, 2), lax.rem(place, 2)

    to_twin = {"dev": 2 * chip + 1 - core}
    across = {"sec": 1 - sec}

    pairs = (
        (queries_hbm, queries),
        (keys_hbm, keys),
        (values_hbm, values),
        (lengths_hbm, lengths),
        (out_proj_hbm, out_proj),
        (residual_hbm, residual),
        (gain_hbm, gain),
        (ids_hbm, ids),
        (router_hbm, router),
        (owners_hbm, owners),
        (gate_hbm.at[0], rising.at[pl.ds(0, units)]),
        (up_hbm.at[0], rising.at[pl.ds(units, units)]),
        (down_hbm.at[0], down_w),
    )
    loads = [
        pltpu.make_async_copy(source, target, load_sem.at[i])
        for i, (source, target) in enumerate(pairs)
    ]
    large = (4, 10, 11, 12)
    for i, load in enumerate(loads):
        if i not in large:
            load.start()

    barrier = pltpu.get_barrier_semaphore()
    pl.semaphore_signal(barrier, inc=1, device_id=across, device_id_type=MESH)

    @pl.loop(1, n_dev)
    def _(k):
        place = {"dev": flipped(dev, k, n_dev)}
        pl.semaphore_signal(barrier, inc=1, device_id=place, device_id_type=MESH)

    def remote(source, target, sent, received, place):
        return pltpu.make_async_remote_copy(
            src_ref=source,
            dst_ref=target,
            send_sem=sent,
            recv_sem=received,
            device_id=place,
            device_id_type=MESH,
        )

    def sending(phase, buffer, k):
        own = buffer.at[core, chip]
        return remote(
            own, own, send_sem.at[phase, k], recv_sem.at[phase, k],
            {"dev": flipped(dev, k, n_dev)},
        )

    def gather_start(phase, buffer):
        @pl.loop(1, n_dev)
        def _(step):
            sending(phase, buffer, n_dev - step).start()

    def landed(phase, buffer, k):
        place, side = device_of(k)
        block = buffer.at[side, place]
        remote(
            block, block, send_sem.at[phase, k], recv_sem.at[phase, k], to_twin
        ).wait_recv()

    def gather_sent(phase, buffer):
        @pl.loop(1, n_dev)
        def _(k):
            sending(phase, buffer, k).wait_send()

    loads[0].wait()
    wide_queries = queries[...].astype(jnp.float32)
    for row in range(rows_here):
        for kv in range(kv_heads):
            for g in range(group):
                start = (kv * group + g) * head_dim
                query_rows[kv, row * group + g : row * group + g + 1, :] = wide_queries[
                    row : row + 1, start : start + head_dim
                ]
    loads[1].wait()
    loads[3].wait()
    loads[2].wait()
    for i in large:
        loads[i].start()
    pl.semaphore_wait(barrier, n_dev)
    position = lax.broadcasted_iota(jnp.int32, (group, span), 1)

    @pl.loop(0, kv_heads)
    def _(kv):
        scores = []
        for row in range(rows_here):
            query = query_rows[kv, row * group : (row + 1) * group, :].astype(jnp.bfloat16)
            found = times_transpose(query, keys[row, kv]) * (1.0 / math.sqrt(head_dim))
            scores.append(jnp.where(position < lengths[row], found, -jnp.inf))
        scores = jnp.concatenate(scores, axis=0)
        raised = jnp.exp(scores - jnp.max(scores, axis=1, keepdims=True))
        probs = (raised / jnp.sum(raised, axis=1, keepdims=True)).astype(jnp.bfloat16)
        for row in range(rows_here):
            found = jnp.dot(
                probs[row * group : (row + 1) * group],
                values[row, kv],
                preferred_element_type=jnp.float32,
            )
            heads_in[kv, core, chip, row] = found.astype(jnp.bfloat16)
        gather_start(kv, heads_in.at[kv])

    for i in (5, 6, 7, 8, 9):
        loads[i].wait()
    named = jnp.int32(0)
    for e in range(owners.shape[0]):
        named = named + jnp.where(owners[e] == dev, jnp.int32(e), jnp.int32(0))
    lying = jnp.sum(jnp.where(ids[...] == named, router[...], 0.0), axis=0, keepdims=True)
    square = (rows, rows)
    diagonal = lax.broadcasted_iota(jnp.int32, square, 0) == lax.broadcasted_iota(
        jnp.int32, square, 1
    )
    weight = jnp.sum(
        jnp.where(diagonal, jnp.broadcast_to(lying, square), 0.0), axis=1, keepdims=True
    )

    loads[4].wait()
    part_sum[...] = jnp.zeros((rows, cols), jnp.float32)

    @pl.loop(0, kv_heads)
    def _(kv):
        @pl.loop(1, n_dev)
        def _(k):
            landed(kv, heads_in.at[kv], k)

        for d in range(n_dev):
            for row in range(rows_here):
                place = (d * rows_here + row) * group
                heads_wide[place : place + group, :] = heads_in[kv, d % 2, d // 2, row].astype(
                    jnp.float32
                )
        features = jnp.concatenate(
            [heads_wide[pl.ds(g, rows, stride=group), :] for g in range(group)], axis=1
        ).astype(jnp.bfloat16)
        start = pl.multiple_of(kv * kv_width, kv_width)
        part_sum[...] += times_transpose(features, out_proj[:, pl.ds(start, kv_width)])

    part = part_sum[...].astype(jnp.bfloat16)
    part_out[...] = part
    swap = remote(part_out, part_in, pair_sem.at[0, 0], pair_sem.at[0, 1], across)
    swap.start()
    swap.wait_recv()
    base = residual[...].astype(jnp.float32) + (
        part.astype(jnp.float32) + part_in[...].astype(jnp.float32)
    )
    hidden_in[core, chip] = base.astype(jnp.bfloat16)
    gather_start(kv_heads, hidden_in)

    loads[10].wait()
    loads[11].wait()
    squares = jnp.zeros((rows, cols), jnp.float32)
    raising = jnp.zeros((rows, 2 * units), jnp.float32)

    batch = n_dev // 4

    def take(k, squares, raising):
        place, side = device_of(k)
        start = pl.multiple_of((2 * place + side) * cols, cols)
        block = hidden_in[side, place].astype(jnp.float32)
        scale = gain[pl.ds(start, cols)].astype(jnp.float32).reshape(1, cols)
        scaled = (block * scale).astype(jnp.bfloat16)
        return (
            squares + block * block,
            raising + times_transpose(scaled, rising[:, pl.ds(start, cols)]),
        )

    def stage(j, carried):
        @pl.when(j > 0)
        def _():
            landed(kv_heads, hidden_in, j * batch)

        @pl.loop(1, batch)
        def _(i):
            landed(kv_heads, hidden_in, j * batch + i)

        for i in range(batch):
            carried = take(j * batch + i, *carried)
        return carried

    squares, raising = lax.fori_loop(0, 4, stage, (squares, raising))
    square_mean = jnp.sum(squares, axis=1, keepdims=True) / (n_dev * cols)
    raising = raising * lax.rsqrt(square_mean + epsilon)
    gate_act, up_act = raising[:, :units], raising[:, units:]
    act = (gate_act * (1.0 / (1.0 + jnp.exp(-gate_act))) * up_act).astype(jnp.bfloat16)

    def lowered(side, k):
        start = pl.multiple_of((2 * chip_of(k) + side) * cols, cols)
        made = jnp.dot(act, down_w[:, pl.ds(start, cols)], preferred_element_type=jnp.float32)
        return made * weight

    loads[12].wait()
    batch = chips // 2

    def crossing(h):
        part = pl.ds(h * batch, batch)
        return remote(
            cross_out.at[part], cross_in.at[part], back_send_sem.at[0, h],
            back_recv_sem.at[0, h], to_twin,
        )

    def backing(k):
        return remote(
            back_out.at[k], back_in.at[k], back_send_sem.at[1, k], back_recv_sem.at[1, k],
            {"dev": 2 * chip_of(k) + core},
        )

    @pl.loop(0, 2)
    def _(step):
        h = 1 - step
        for i in range(batch):
            k = h * batch + i
            cross_out[k] = lowered(1 - core, k).astype(jnp.bfloat16)
        crossing(h).start()

    @pl.loop(0, 2)
    def _(step):
        h = 1 - step
        made = [lowered(core, h * batch + i) for i in range(batch)]
        crossing(h).wait_recv()
        for i in range(batch):
            k = h * batch + i
            back_out[k] = (made[i] + cross_in[k].astype(jnp.float32)).astype(jnp.bfloat16)

        @pl.loop(h * batch + step, (h + 1) * batch)
        def _(k):
            backing(k).start()

    @pl.loop(0, kv_heads)
    def _(kv):
        gather_sent(kv, heads_in.at[kv])

    gather_sent(kv_heads, hidden_in)
    swap.wait_send()

    @pl.loop(0, 2)
    def _(h):
        crossing(h).wait_send()

    def collect(k, moe):
        backing(k).wait_recv()
        return moe + back_in[k].astype(jnp.float32)

    moe = lax.fori_loop(1, chips, collect, back_out[0].astype(jnp.float32))
    moe = moe.astype(jnp.bfloat16)
    last_out[...] = moe
    last = remote(last_out, last_in, pair_sem.at[1, 0], pair_sem.at[1, 1], across)
    last.start()

    @pl.loop(1, chips)
    def _(k):
        backing(k).wait_send()

    last.wait_send()
    last.wait_recv()
    output[...] = (
        base + (moe.astype(jnp.float32) + last_in[...].astype(jnp.float32))
    ).astype(jnp.bfloat16)


def fused(
    n_dev,
    queries,
    cache_keys,
    cache_values,
    lengths,
    out_proj,
    residual,
    norm_gain,
    expert_ids,
    gate_weights,
    owners,
    gate_proj,
    up_proj,
    down_proj,
):
    rows_here, kv_heads, span, head_dim = cache_keys.shape
    cols = out_proj.shape[0]
    rows, width = residual.shape[0], norm_gain.shape[0]
    group = queries.shape[1] // (kv_heads * head_dim)
    units = gate_proj.shape[1]
    chips = n_dev // 2
    whole = pl.BlockSpec(memory_space=pltpu.HBM)
    wide, narrow = jnp.float32, jnp.bfloat16
    gain = norm_gain
    operands = (
        queries,
        lengths,
        residual,
        gain,
        expert_ids.T,
        gate_weights.T,
        owners,
        cache_keys,
        cache_values,
        out_proj,
        gate_proj,
        up_proj,
        down_proj,
    )
    return pl.pallas_call(
        functools.partial(fused_kernel, n_dev),
        out_shape=pltpu.VMEM((rows, cols), narrow),
        in_specs=[whole] * 13,
        out_specs=pl.BlockSpec(memory_space=pltpu.VMEM),
        scratch_shapes=[
            pltpu.VMEM(queries.shape, narrow),
            pltpu.SMEM(lengths.shape, jnp.int32),
            pltpu.VMEM(residual.shape, narrow),
            pltpu.VMEM(gain.shape, narrow),
            pltpu.VMEM(expert_ids.shape[::-1], jnp.int32),
            pltpu.VMEM(gate_weights.shape[::-1], wide),
            pltpu.SMEM(owners.shape, jnp.int32),
            pltpu.VMEM(cache_keys.shape, narrow),
            pltpu.VMEM(cache_values.shape, narrow),
            pltpu.VMEM(out_proj.shape, narrow),
            pltpu.VMEM((2 * units, width), narrow),
            pltpu.VMEM((units, width), narrow),
            pltpu.VMEM((kv_heads, rows_here * group, head_dim), wide),
            pltpu.VMEM((kv_heads, 2, chips, rows_here, group, head_dim), narrow),
            pltpu.VMEM((rows * group, head_dim), wide),
            pltpu.VMEM((rows, cols), wide),
            pltpu.VMEM((rows, cols), narrow),
            pltpu.VMEM((rows, cols), narrow),
            pltpu.VMEM((2, chips, rows, cols), narrow),
            pltpu.VMEM((chips, rows, cols), narrow),
            pltpu.VMEM((chips, rows, cols), narrow),
            pltpu.VMEM((chips, rows, cols), narrow),
            pltpu.VMEM((chips, rows, cols), narrow),
            pltpu.VMEM((rows, cols), narrow),
            pltpu.VMEM((rows, cols), narrow),
            pltpu.SemaphoreType.DMA((13,)),
            pltpu.SemaphoreType.DMA((kv_heads + 1, n_dev)),
            pltpu.SemaphoreType.DMA((kv_heads + 1, n_dev)),
            pltpu.SemaphoreType.DMA((2, chips)),
            pltpu.SemaphoreType.DMA((2, chips)),
            pltpu.SemaphoreType.DMA((2, 2)),
        ],
        compiler_params=pltpu.CompilerParams(
            collective_id=0, has_side_effects=True, vmem_limit_bytes=VMEM_LIMIT
        ),
        cost_estimate=pl.CostEstimate(
            flops=2 * rows * width * (width + 3 * units),
            bytes_accessed=2 * width * (width + 3 * units),
            transcendentals=0,
        ),
    )(*(pltpu.with_memory_space_constraint(operand, pltpu.HBM) for operand in operands))


def tiles_whole(mesh, operands):
    queries, cache_keys, _, _, out_proj, residual = operands[:6]
    owners, gate_proj = operands[9], operands[10]
    group = queries.shape[1] // (cache_keys.shape[1] * cache_keys.shape[3])
    return (
        mesh.shape["sec"] == 2
        and mesh.shape["dev"] in (4, 8, 16)
        and owners.shape[0] == mesh.shape["dev"]
        and gate_proj.shape[0] == 1
        and group % 16 == 0
        and cache_keys.shape[3] % 128 == 0
        and cache_keys.shape[2] % 128 == 0
        and residual.shape[0] % 16 == 0
        and out_proj.shape[0] % 128 == 0
        and gate_proj.shape[1] % 128 == 0
    )


def solution(mesh):
    in_specs = (
        P("dev", "sec"),
        P("dev", "sec", None, None),
        P("dev", "sec", None, None),
        P("dev"),
        P("dev", "sec"),
        P(None, "dev"),
        P(),
        P(),
        P(),
        P(),
        P("dev", "sec", None),
        P("dev", "sec", None),
        P("dev", "sec", None),
    )
    out_specs = P(None, "dev")

    def chosen(*operands):
        if tiles_whole(mesh, operands):
            return fused(mesh.shape["dev"], *operands)
        return shards(*operands)

    return jax.shard_map(chosen, mesh=mesh, in_specs=in_specs, out_specs=out_specs, check_vma=False)
```

```python
import functools
import math

import jax
import jax.numpy as jnp
from jax import lax
from jax.experimental import pallas as pl
from jax.experimental.pallas import tpu as pltpu
from jax.sharding import PartitionSpec as P

epsilon = 1e-05
MESH = pl.DeviceIdType.MESH


def slot_targets(expert_ids, owners, capacity):
    experts = owners.shape[0]
    flat_ids = expert_ids.reshape(-1)
    one_hot = (flat_ids[:, None] == jnp.arange(experts, dtype=jnp.int32)[None, :]).astype(jnp.int32)
    before = jnp.cumsum(one_hot, axis=0) - one_hot
    position = jnp.sum(before * one_hot, axis=1)
    holder = jnp.sum(one_hot * owners[None, :], axis=1)
    return (holder * capacity + position).reshape(expert_ids.shape)


def routing_tables(expert_ids, gate_weights, owners, capacity):
    target = slot_targets(expert_ids, owners, capacity)
    places = jnp.arange(owners.shape[0] * capacity, dtype=jnp.int32)
    matched = target[None, :, :] == places[:, None, None]
    sending = jnp.any(matched, axis=2)
    weighting = jnp.sum(
        jnp.where(matched, gate_weights[None, :, :], jnp.zeros_like(gate_weights)[None, :, :]),
        axis=2,
    )
    return (sending, weighting)


def times_transpose(left, right):
    return lax.dot_general(
        left, right, (((1,), (1,)), ((), ())), preferred_element_type=jnp.float32
    )


def attend(queries, cache_keys, cache_values, lengths):
    rows, kv_heads, key_span, head_dim = cache_keys.shape
    group_size = queries.shape[1] // (kv_heads * head_dim)
    grouped = queries.reshape(rows, kv_heads, group_size, head_dim)
    scores = jnp.einsum(
        "rkgd,rktd->rkgt", grouped, cache_keys, preferred_element_type=jnp.float32
    ) / math.sqrt(head_dim)
    live_mask = (
        jnp.arange(key_span, dtype=jnp.int32)[None, None, None, :] < lengths[:, None, None, None]
    )
    scores = jnp.where(live_mask, scores, -jnp.inf)
    row_top = jnp.max(scores, axis=-1, keepdims=True)
    raised = jnp.exp(scores - row_top)
    soft_weight = (raised / jnp.sum(raised, axis=-1, keepdims=True)).astype(jnp.bfloat16)
    head_out = jnp.einsum(
        "rkgt,rktd->rkgd", soft_weight, cache_values, preferred_element_type=jnp.float32
    )
    return head_out.astype(jnp.bfloat16).reshape(rows, -1)


def root_norm(arrived, norm_gain):
    square_mean = jnp.mean(arrived * arrived, axis=-1, keepdims=True)
    return (arrived * lax.rsqrt(square_mean + epsilon) * norm_gain.astype(jnp.float32)).astype(
        jnp.bfloat16
    )


def expert_ffn(normed, gate_w, up_w, down_w):
    gate_act = times_transpose(normed, gate_w)
    up_act = times_transpose(normed, up_w)
    hidden = (jax.nn.silu(gate_act) * up_act).astype(jnp.bfloat16)
    return jnp.dot(hidden, down_w, preferred_element_type=jnp.float32)


def shards(
    queries,
    cache_keys,
    cache_values,
    lengths,
    out_proj,
    residual,
    norm_gain,
    expert_ids,
    gate_weights,
    owners,
    gate_proj,
    up_proj,
    down_proj,
):
    head_out = attend(queries, cache_keys, cache_values, lengths)
    attention_part = times_transpose(lax.all_gather(head_out, "dev", axis=0, tiled=True), out_proj)
    rows_all, top_count = expert_ids.shape
    experts = owners.shape[0]
    capacity = min(rows_all, 3 * top_count * rows_all // experts)
    col_count = out_proj.shape[0]
    sending, weighting = routing_tables(expert_ids, gate_weights, owners, capacity)
    residual_wide = residual.astype(jnp.float32)
    attention_out = lax.psum(attention_part, "sec")
    hidden_in = (residual_wide + attention_out).astype(jnp.bfloat16)
    outbound = jnp.dot(sending.astype(jnp.bfloat16), hidden_in, preferred_element_type=jnp.float32)
    outbound = outbound.astype(jnp.bfloat16).reshape(experts, capacity, col_count)
    inbound = lax.all_to_all(outbound, "dev", split_axis=0, concat_axis=2, tiled=True)
    arrived = inbound[0].astype(jnp.float32)
    normed = root_norm(arrived, norm_gain)
    expert_out = expert_ffn(normed, gate_proj[0], up_proj[0], down_proj[0])
    place_weight = jnp.sum(weighting, axis=1)
    own_weight = lax.dynamic_slice_in_dim(
        place_weight, lax.axis_index("dev") * capacity, capacity, 0
    )
    weighted = (expert_out * own_weight[:, None]).astype(jnp.bfloat16)
    returned = lax.all_to_all(
        weighted.reshape(1, capacity, weighted.shape[1]),
        "dev",
        split_axis=2,
        concat_axis=0,
        tiled=True,
    )
    moe = jnp.dot(
        sending.T.astype(jnp.bfloat16),
        returned.reshape(-1, col_count),
        preferred_element_type=jnp.float32,
    )
    summed = lax.psum(moe, "sec")
    return (residual_wide + attention_out + summed).astype(jnp.bfloat16)
VMEM_LIMIT = 32 * 1024 * 1024


def fused_kernel(
    n_dev,
    queries_hbm,
    lengths_hbm,
    residual_hbm,
    gain_hbm,
    ids_hbm,
    router_hbm,
    owners_hbm,
    keys_hbm,
    values_hbm,
    out_proj_hbm,
    gate_hbm,
    up_hbm,
    down_hbm,
    output,
    queries,
    lengths,
    residual,
    gain,
    ids,
    router,
    owners,
    keys,
    values,
    out_proj,
    rising,
    down_w,
    query_rows,
    heads_in,
    heads_wide,
    part_sum,
    part_out,
    part_in,
    hidden_in,
    cross_out,
    cross_in,
    back_out,
    back_in,
    last_out,
    last_in,
    load_sem,
    send_sem,
    recv_sem,
    pass_sem,
    pair_recv_sem,
    back_send_sem,
    back_recv_sem,
    pair_sem,
):
    sec = lax.axis_index("sec")
    dev = lax.axis_index("dev")
    chip, core = lax.div(dev, 2), lax.rem(dev, 2)
    chips = n_dev // 2
    rows_here, kv_heads, span, head_dim = keys.shape
    group = query_rows.shape[1] // rows_here
    rows = n_dev * rows_here
    cols = out_proj.shape[0]
    units = down_w.shape[0]
    kv_width = group * head_dim

    def flipped(place, k, amount):
        bit, result = 1, 0
        while bit < amount:
            result = result + lax.rem(lax.div(place, bit) + k // bit, 2) * bit
            bit *= 2
        return result

    def chip_of(k):
        return flipped(chip, k, chips)

    def pair_of(p):
        return pl.ds(2 * flipped(lax.div(chip, 2), p, chips // 2), 2)

    to_twin = {"dev": 2 * chip + 1 - core}
    across = {"sec": 1 - sec}

    pairs = (
        (queries_hbm, queries),
        (keys_hbm, keys),
        (values_hbm, values),
        (lengths_hbm, lengths),
        (out_proj_hbm, out_proj),
        (residual_hbm, residual),
        (gain_hbm, gain),
        (ids_hbm, ids),
        (router_hbm, router),
        (owners_hbm, owners),
        (gate_hbm.at[0], rising.at[pl.ds(0, units)]),
        (up_hbm.at[0], rising.at[pl.ds(units, units)]),
        (down_hbm.at[0], down_w),
    )
    loads = [
        pltpu.make_async_copy(source, target, load_sem.at[i])
        for i, (source, target) in enumerate(pairs)
    ]
    large = (4, 10, 11, 12)
    for i, load in enumerate(loads):
        if i not in large:
            load.start()

    barrier = pltpu.get_barrier_semaphore()
    for place in (across, to_twin):
        pl.semaphore_signal(barrier, inc=1, device_id=place, device_id_type=MESH)

    @pl.loop(1, chips)
    def _(k):
        place = {"dev": 2 * chip_of(k) + core}
        pl.semaphore_signal(barrier, inc=1, device_id=place, device_id_type=MESH)

    def remote(source, target, sent, received, place):
        return pltpu.make_async_remote_copy(
            src_ref=source,
            dst_ref=target,
            send_sem=sent,
            recv_sem=received,
            device_id=place,
            device_id_type=MESH,
        )

    def sending(phase, buffer, k):
        own = buffer.at[core, chip]
        return remote(
            own, own, send_sem.at[phase, k], recv_sem.at[phase, chip],
            {"dev": 2 * chip_of(k) + core},
        )

    def gather_start(phase, buffer):
        @pl.loop(1, chips)
        def _(step):
            sending(phase, buffer, chips - step).start()

    def passing(phase, buffer, p):
        pair = buffer.at[core, pair_of(p)]
        return remote(pair, pair, pass_sem.at[phase, p], pair_recv_sem.at[phase, p], to_twin)

    def arriving(phase, buffer, k):
        block = buffer.at[core, chip_of(k)]
        remote(
            block, block, send_sem.at[phase, 0], recv_sem.at[phase, chip_of(k)], to_twin
        ).wait_recv()

    def gather_pass(phase, buffer, p):
        for k in (2 * p, 2 * p + 1):
            if not isinstance(k, int) or k:
                arriving(phase, buffer, k)
        passing(phase, buffer, p).start()

    def landed(phase, buffer, p):
        pair = buffer.at[1 - core, pair_of(p)]
        remote(
            pair, pair, pass_sem.at[phase, p], pair_recv_sem.at[phase, p], to_twin
        ).wait_recv()

    def gather_sent(phase, buffer):
        @pl.loop(1, chips)
        def _(k):
            sending(phase, buffer, k).wait_send()

        @pl.loop(0, chips // 2)
        def _(p):
            passing(phase, buffer, p).wait_send()

    loads[0].wait()
    wide_queries = queries[...].astype(jnp.float32)
    for row in range(rows_here):
        for kv in range(kv_heads):
            for g in range(group):
                start = (kv * group + g) * head_dim
                query_rows[kv, row * group + g : row * group + g + 1, :] = wide_queries[
                    row : row + 1, start : start + head_dim
                ]
    loads[1].wait()
    loads[3].wait()
    loads[2].wait()
    for i in large:
        loads[i].start()
    pl.semaphore_wait(barrier, chips + 1)
    position = lax.broadcasted_iota(jnp.int32, (group, span), 1)

    @pl.loop(0, kv_heads)
    def _(kv):
        scores = []
        for row in range(rows_here):
            query = query_rows[kv, row * group : (row + 1) * group, :].astype(jnp.bfloat16)
            found = times_transpose(query, keys[row, kv]) * (1.0 / math.sqrt(head_dim))
            scores.append(jnp.where(position < lengths[row], found, -jnp.inf))
        scores = jnp.concatenate(scores, axis=0)
        raised = jnp.exp(scores - jnp.max(scores, axis=1, keepdims=True))
        probs = (raised / jnp.sum(raised, axis=1, keepdims=True)).astype(jnp.bfloat16)
        for row in range(rows_here):
            found = jnp.dot(
                probs[row * group : (row + 1) * group],
                values[row, kv],
                preferred_element_type=jnp.float32,
            )
            heads_in[kv, core, chip, row] = found.astype(jnp.bfloat16)
        gather_start(kv, heads_in.at[kv])

    for i in (5, 6, 7, 8, 9):
        loads[i].wait()
    named = jnp.int32(0)
    for e in range(owners.shape[0]):
        named = named + jnp.where(owners[e] == dev, jnp.int32(e), jnp.int32(0))
    lying = jnp.sum(jnp.where(ids[...] == named, router[...], 0.0), axis=0, keepdims=True)
    square = (rows, rows)
    diagonal = lax.broadcasted_iota(jnp.int32, square, 0) == lax.broadcasted_iota(
        jnp.int32, square, 1
    )
    weight = jnp.sum(
        jnp.where(diagonal, jnp.broadcast_to(lying, square), 0.0), axis=1, keepdims=True
    )

    @pl.loop(0, kv_heads)
    def _(kv):
        gather_pass(kv, heads_in.at[kv], 0)

        @pl.loop(1, chips // 2)
        def _(p):
            gather_pass(kv, heads_in.at[kv], p)

    loads[4].wait()
    part_sum[...] = jnp.zeros((rows, cols), jnp.float32)

    @pl.loop(0, kv_heads)
    def _(kv):
        @pl.loop(0, chips // 2)
        def _(p):
            landed(kv, heads_in.at[kv], p)

        for d in range(n_dev):
            for row in range(rows_here):
                place = (d * rows_here + row) * group
                heads_wide[place : place + group, :] = heads_in[kv, d % 2, d // 2, row].astype(
                    jnp.float32
                )
        features = jnp.concatenate(
            [heads_wide[pl.ds(g, rows, stride=group), :] for g in range(group)], axis=1
        ).astype(jnp.bfloat16)
        start = pl.multiple_of(kv * kv_width, kv_width)
        part_sum[...] += times_transpose(features, out_proj[:, pl.ds(start, kv_width)])

    part = part_sum[...].astype(jnp.bfloat16)
    part_out[...] = part
    swap = remote(part_out, part_in, pair_sem.at[0, 0], pair_sem.at[0, 1], across)
    swap.start()
    swap.wait_recv()
    base = residual[...].astype(jnp.float32) + (
        part.astype(jnp.float32) + part_in[...].astype(jnp.float32)
    )
    hidden_in[core, chip] = base.astype(jnp.bfloat16)
    gather_start(kv_heads, hidden_in)

    loads[10].wait()
    loads[11].wait()
    squares = jnp.zeros((rows, cols), jnp.float32)
    raising = jnp.zeros((rows, 2 * units), jnp.float32)

    def take(side, p, squares, raising):
        first = pair_of(p).start
        for half in range(2):
            start = pl.multiple_of((2 * (first + half) + side) * cols, cols)
            block = hidden_in[side, first + half].astype(jnp.float32)
            scale = gain[pl.ds(start, cols)].astype(jnp.float32).reshape(1, cols)
            scaled = (block * scale).astype(jnp.bfloat16)
            squares = squares + block * block
            raising = raising + times_transpose(scaled, rising[:, pl.ds(start, cols)])
        return squares, raising

    gather_pass(kv_heads, hidden_in, 0)
    squares, raising = take(core, 0, squares, raising)

    def stage(p, carried):
        gather_pass(kv_heads, hidden_in, p)
        landed(kv_heads, hidden_in, p - 1)
        return take(1 - core, p - 1, *take(core, p, *carried))

    squares, raising = lax.fori_loop(1, chips // 2, stage, (squares, raising))
    landed(kv_heads, hidden_in, chips // 2 - 1)
    squares, raising = take(1 - core, chips // 2 - 1, squares, raising)
    square_mean = jnp.sum(squares, axis=1, keepdims=True) / (n_dev * cols)
    raising = raising * lax.rsqrt(square_mean + epsilon)
    gate_act, up_act = raising[:, :units], raising[:, units:]
    act = (gate_act * (1.0 / (1.0 + jnp.exp(-gate_act))) * up_act).astype(jnp.bfloat16)

    def lowered(side, k):
        start = pl.multiple_of((2 * chip_of(k) + side) * cols, cols)
        made = jnp.dot(act, down_w[:, pl.ds(start, cols)], preferred_element_type=jnp.float32)
        return made * weight

    loads[12].wait()
    batch = chips // 4

    def crossing(h):
        part = pl.ds(h * batch, batch)
        return remote(
            cross_out.at[part], cross_in.at[part], back_send_sem.at[0, h],
            back_recv_sem.at[0, h], to_twin,
        )

    def backing(k):
        return remote(
            back_out.at[k], back_in.at[k], back_send_sem.at[1, k], back_recv_sem.at[1, k],
            {"dev": 2 * chip_of(k) + core},
        )

    @pl.loop(0, 4)
    def _(step):
        h = 3 - step
        for i in range(batch):
            k = h * batch + i
            cross_out[k] = lowered(1 - core, k).astype(jnp.bfloat16)
        crossing(h).start()

    @pl.loop(0, 4)
    def _(step):
        h = 3 - step
        made = [lowered(core, h * batch + i) for i in range(batch)]
        crossing(h).wait_recv()
        for i in range(batch):
            k = h * batch + i
            back_out[k] = (made[i] + cross_in[k].astype(jnp.float32)).astype(jnp.bfloat16)

        @pl.loop(h * batch + lax.div(step, 3), (h + 1) * batch)
        def _(k):
            backing(k).start()

    @pl.loop(0, kv_heads)
    def _(kv):
        gather_sent(kv, heads_in.at[kv])

    gather_sent(kv_heads, hidden_in)
    swap.wait_send()

    @pl.loop(0, 4)
    def _(h):
        crossing(h).wait_send()

    def collect(k, moe):
        backing(k).wait_recv()
        return moe + back_in[k].astype(jnp.float32)

    moe = lax.fori_loop(1, chips, collect, back_out[0].astype(jnp.float32))
    moe = moe.astype(jnp.bfloat16)
    last_out[...] = moe
    last = remote(last_out, last_in, pair_sem.at[1, 0], pair_sem.at[1, 1], across)
    last.start()

    @pl.loop(1, chips)
    def _(k):
        backing(k).wait_send()

    last.wait_send()
    last.wait_recv()
    output[...] = (
        base + (moe.astype(jnp.float32) + last_in[...].astype(jnp.float32))
    ).astype(jnp.bfloat16)


def fused(
    n_dev,
    queries,
    cache_keys,
    cache_values,
    lengths,
    out_proj,
    residual,
    norm_gain,
    expert_ids,
    gate_weights,
    owners,
    gate_proj,
    up_proj,
    down_proj,
):
    rows_here, kv_heads, span, head_dim = cache_keys.shape
    cols = out_proj.shape[0]
    rows, width = residual.shape[0], norm_gain.shape[0]
    group = queries.shape[1] // (kv_heads * head_dim)
    units = gate_proj.shape[1]
    chips = n_dev // 2
    whole = pl.BlockSpec(memory_space=pltpu.HBM)
    wide, narrow = jnp.float32, jnp.bfloat16
    gain = norm_gain
    operands = (
        queries,
        lengths,
        residual,
        gain,
        expert_ids.T,
        gate_weights.T,
        owners,
        cache_keys,
        cache_values,
        out_proj,
        gate_proj,
        up_proj,
        down_proj,
    )
    return pl.pallas_call(
        functools.partial(fused_kernel, n_dev),
        out_shape=pltpu.VMEM((rows, cols), narrow),
        in_specs=[whole] * 13,
        out_specs=pl.BlockSpec(memory_space=pltpu.VMEM),
        scratch_shapes=[
            pltpu.VMEM(queries.shape, narrow),
            pltpu.SMEM(lengths.shape, jnp.int32),
            pltpu.VMEM(residual.shape, narrow),
            pltpu.VMEM(gain.shape, narrow),
            pltpu.VMEM(expert_ids.shape[::-1], jnp.int32),
            pltpu.VMEM(gate_weights.shape[::-1], wide),
            pltpu.SMEM(owners.shape, jnp.int32),
            pltpu.VMEM(cache_keys.shape, narrow),
            pltpu.VMEM(cache_values.shape, narrow),
            pltpu.VMEM(out_proj.shape, narrow),
            pltpu.VMEM((2 * units, width), narrow),
            pltpu.VMEM((units, width), narrow),
            pltpu.VMEM((kv_heads, rows_here * group, head_dim), wide),
            pltpu.VMEM((kv_heads, 2, chips, rows_here, group, head_dim), narrow),
            pltpu.VMEM((rows * group, head_dim), wide),
            pltpu.VMEM((rows, cols), wide),
            pltpu.VMEM((rows, cols), narrow),
            pltpu.VMEM((rows, cols), narrow),
            pltpu.VMEM((2, chips, rows, cols), narrow),
            pltpu.VMEM((chips, rows, cols), narrow),
            pltpu.VMEM((chips, rows, cols), narrow),
            pltpu.VMEM((chips, rows, cols), narrow),
            pltpu.VMEM((chips, rows, cols), narrow),
            pltpu.VMEM((rows, cols), narrow),
            pltpu.VMEM((rows, cols), narrow),
            pltpu.SemaphoreType.DMA((13,)),
            pltpu.SemaphoreType.DMA((kv_heads + 1, chips)),
            pltpu.SemaphoreType.DMA((kv_heads + 1, chips)),
            pltpu.SemaphoreType.DMA((kv_heads + 1, chips // 2)),
            pltpu.SemaphoreType.DMA((kv_heads + 1, chips // 2)),
            pltpu.SemaphoreType.DMA((2, chips)),
            pltpu.SemaphoreType.DMA((2, chips)),
            pltpu.SemaphoreType.DMA((2, 2)),
        ],
        compiler_params=pltpu.CompilerParams(
            collective_id=0, has_side_effects=True, vmem_limit_bytes=VMEM_LIMIT
        ),
        cost_estimate=pl.CostEstimate(
            flops=2 * rows * width * (width + 3 * units),
            bytes_accessed=2 * width * (width + 3 * units),
            transcendentals=0,
        ),
    )(*(pltpu.with_memory_space_constraint(operand, pltpu.HBM) for operand in operands))


def tiles_whole(mesh, operands):
    queries, cache_keys, _, _, out_proj, residual = operands[:6]
    owners, gate_proj = operands[9], operands[10]
    group = queries.shape[1] // (cache_keys.shape[1] * cache_keys.shape[3])
    return (
        mesh.shape["sec"] == 2
        and mesh.shape["dev"] in (8, 16)
        and owners.shape[0] == mesh.shape["dev"]
        and gate_proj.shape[0] == 1
        and group % 16 == 0
        and cache_keys.shape[3] % 128 == 0
        and cache_keys.shape[2] % 128 == 0
        and residual.shape[0] % 16 == 0
        and out_proj.shape[0] % 128 == 0
        and gate_proj.shape[1] % 128 == 0
    )


def solution(mesh):
    in_specs = (
        P("dev", "sec"),
        P("dev", "sec", None, None),
        P("dev", "sec", None, None),
        P("dev"),
        P("dev", "sec"),
        P(None, "dev"),
        P(),
        P(),
        P(),
        P(),
        P("dev", "sec", None),
        P("dev", "sec", None),
        P("dev", "sec", None),
    )
    out_specs = P(None, "dev")

    def chosen(*operands):
        if tiles_whole(mesh, operands):
            return fused(mesh.shape["dev"], *operands)
        return shards(*operands)

    return jax.shard_map(chosen, mesh=mesh, in_specs=in_specs, out_specs=out_specs, check_vma=False)
```
